256 devices in a mesh: ctx: 32 (over y, x, core), tp: 8 (over z).
Axes of the slice: x: 4, y: 4, z: 8, core: 2. Of those that a mesh axis runs over, the one named last changes fastest.
Arguments:
- hidden: bfloat16 [256, 8192], P('ctx', 'tp')
- norm_gain: float32 [8192], replicated, may hold values from 0.5 to 1.5
- head_weight: bfloat16 [128256, 8192], P(('ctx', 'tp'))
- targets: int32 [256], replicated, may hold values from 0 to 128255
- ref_logprobs: float32 [256], P('ctx'), may hold values from -22 to -10
- block_order: int32 [64], P('ctx'), may hold values from 0 to 63, each once
- lengths: int32 [2], replicated, may hold values from 32 to 128
Outputs:
- loss: float32 [], replicated
- hidden_grad: bfloat16 [256, 8192], P('ctx', 'tp')
The draws below stay inside these ranges and needn't reach their ends.
Inputs may be any that keep to these rules, and one draw needn't show every extreme that they name: `block_order`: each block number appears once.
All inputs are finite; a program needn't handle non-finite values.
Results may differ from the reference program's by a relative error of at most 0.0034.
Values may be sent and summed in bfloat16 or wider, within the bound.
No kernel may reach another device: no remote copies, remote signals or barrier semaphores. Data moves between devices by JAX's collectives and lax.ppermute only.
A program may use at most 64 MiB of HBM per device.

```python
import math
import jax
import jax.numpy as jnp
import numpy as np
from jax import lax

D = 8192
V = 128256
TOK_DEV = 8
BLOCK = 2
TOKENS = 256
SEQ = 128
N_CTX = 32


def special_pairs(key):
    lower = jax.random.permutation(jax.random.fold_in(key, 11), V // 2)[:8].astype(jnp.int32)
    return jnp.stack([lower, lower + V // 2], axis=1)


def head_row(key, index):
    return jax.random.normal(jax.random.fold_in(jax.random.fold_in(key, 101), index), (D,), jnp.float32)


def pair_rows(key):
    pairs = special_pairs(key)
    first = jax.vmap(lambda index: head_row(key, index))(pairs[:, 0])
    other = jax.vmap(lambda index: head_row(key, index))(pairs[:, 1])
    along = jnp.sum(other * first, axis=1, keepdims=True) / jnp.sum(first * first, axis=1, keepdims=True)
    apart = other - along * first
    return (pairs, first, apart)


def draw_head_weight(key, part):
    indices = jnp.arange(V, dtype=jnp.int32)
    table = jax.vmap(lambda index: head_row(key, index))(indices) * (3.0 / math.sqrt(D))
    pairs, first, apart = pair_rows(key)
    levels = jnp.array([110.0, 130.0, 150.0, 170.0, 190.0, 210.0, 225.0, 240.0], jnp.float32)[:, None]
    coef = levels / D
    table = table.at[pairs[:, 0]].set(coef * first)
    table = table.at[pairs[:, 1]].set(coef * (0.99 * first + 0.2 * apart))
    return table.astype(jnp.bfloat16)


def draw_hidden(key, part):
    pairs, first, apart = pair_rows(key)
    own_key = jax.random.fold_in(key, 5)
    noise_key, row_key, col_key = jax.random.split(own_key, 3)
    row_scale = jnp.exp(jax.random.uniform(row_key, (TOKENS, 1), jnp.float32, math.log(0.3), math.log(3.0)))
    col_scale = jnp.exp(jax.random.uniform(col_key, (1, D), jnp.float32, math.log(0.5), math.log(2.0)))
    noise = jax.random.normal(noise_key, (TOKENS, D), jnp.float32)
    values = noise * row_scale * col_scale
    row_slots = jnp.arange(8, dtype=jnp.int32) * (TOKENS // 8)
    values = values.at[row_slots].set(first)
    return values.astype(jnp.bfloat16)


def place_ends(entries, key, low, top_value):
    dims = entries.shape
    index_at = [jax.random.randint(jax.random.fold_in(key, axis), (), 0, dims[axis]) for axis in range(len(dims))]
    entries = entries.at[tuple(index_at)].set(low)
    longest = dims.index(max(dims))
    index_at[longest] = (index_at[longest] + 1) % dims[longest]
    return entries.at[tuple(index_at)].set(top_value)


def block_levels(rng, extent, shards, least, largest):
    factor_of, own = 1.0, jax.random.fold_in(rng, 6)
    for dim, shards_of in shards:
        draws = jnp.exp(jax.random.uniform(jax.random.fold_in(own, dim), (shards_of,), jnp.float32, least / len(shards), largest / len(shards)))
        factor_of = factor_of * jnp.repeat(draws, extent[dim] // shards_of).reshape([-1 if axis == dim else 1 for axis in range(len(extent))])
    return factor_of


def skewed_wide(rng, shape, number_of, lean):
    portions = [min(1 << octave, number_of + 1 - (1 << octave)) * (1 << 20) // math.isqrt((1 << octave) ** lean) + 1 for octave in range((number_of + 1).bit_length()) if 1 << octave <= number_of]
    deviation = 1 + sum(portions) // (1 << 30)
    listing = np.cumsum(np.array([max(1, weight // deviation) for weight in portions]))
    pick = jax.random.randint(jax.random.fold_in(rng, 1), shape, 0, int(listing[len(portions) - 1]))
    start = jnp.left_shift(1, jnp.searchsorted(jnp.asarray(listing, jnp.int32), pick, side="right").astype(jnp.int32))
    standing = start - 1 + jax.random.randint(jax.random.fold_in(rng, 4), shape, 0, 1 << 30) % jnp.minimum(start, number_of + 1 - start)
    return jax.random.permutation(jax.random.fold_in(rng, 2), number_of)[standing].astype(jnp.int32)


def setup_inputs(seed: int = 0) -> dict:
    key_of = jax.random.split(jax.random.key(seed), 8)
    hidden = draw_hidden(jax.random.fold_in(key_of[7], 71), 0)
    norm_gain = jnp.clip(1.0 + 0.1 * jax.random.normal(key_of[1], (D,), jnp.float32), 0.5, 1.5)
    head_weight = draw_head_weight(jax.random.fold_in(key_of[7], 71), 0)
    targets = place_ends(skewed_wide(key_of[3], (TOKENS,), V, 2), jax.random.fold_in(key_of[3], 3), 0, V - 1).astype(jnp.int32)
    ref_logprobs = jnp.clip(-22.0 + 12.0 * jax.random.uniform(key_of[4], (TOKENS,), jnp.float32) ** block_levels(key_of[4], (TOKENS,), ((0, 32),), -0.2, 0.2), -22.0, -10.0)
    block_order = jax.random.permutation(key_of[5], 2 * N_CTX).astype(jnp.int32)
    lengths = jax.random.randint(key_of[6], (2,), SEQ // 4, SEQ + 1).astype(jnp.int32)
    return {"hidden": hidden, "norm_gain": norm_gain, "head_weight": head_weight, "targets": targets, "ref_logprobs": ref_logprobs, "block_order": block_order, "lengths": lengths}


EPSILON = 1e-05
DPO_BETA = 0.05
LOSS_SCALE = 4096.0

def row_layout(block_order, lengths):
    row_ids = jnp.arange(TOKENS, dtype=jnp.int32)
    device = row_ids // TOK_DEV
    within = row_ids % TOK_DEV
    seq_index = within // (2 * BLOCK)
    half_index = within // BLOCK % 2
    offset = within % BLOCK
    position = block_order[2 * device + half_index] * BLOCK + offset
    live_mask = (position < lengths[seq_index]).astype(jnp.float32)
    seq_sign = 1.0 - 2.0 * seq_index.astype(jnp.float32)
    return (live_mask, seq_sign)

def reference(hidden, norm_gain, head_weight, targets, ref_logprobs, block_order, lengths):
    hidden_f32 = hidden.astype(jnp.float32)
    inv_rms = lax.rsqrt(lax.optimization_barrier(jnp.mean(hidden_f32 * hidden_f32, axis=1)) + EPSILON)
    normed = (hidden_f32 * inv_rms[:, None] * norm_gain[None, :]).astype(jnp.bfloat16)
    logits = lax.dot_general(normed, head_weight, (((1,), (1,)), ((), ())), preferred_element_type=jnp.float32)
    row_top = lax.optimization_barrier(jnp.max(logits, axis=1))
    row_total = lax.optimization_barrier(jnp.sum(jnp.exp(logits - row_top[:, None]), axis=1))
    log_total = row_top + jnp.log(row_total)
    picked = jnp.take_along_axis(logits, targets[:, None].astype(jnp.int32), axis=1)[:, 0]
    logprobs = picked - log_total
    live_mask, seq_sign = row_layout(block_order, lengths)
    log_ratio = (logprobs - ref_logprobs) * live_mask
    margin = jnp.sum(log_ratio * seq_sign)
    loss = jax.nn.softplus(-DPO_BETA * margin)
    slope_coef = -DPO_BETA * jax.nn.sigmoid(-DPO_BETA * margin)
    row_grad = slope_coef * seq_sign * live_mask
    columns = lax.broadcasted_iota(jnp.int32, logits.shape, 1)
    onehot = (columns == targets[:, None]).astype(jnp.float32)
    shifted = (onehot - jnp.exp(logits - log_total[:, None])).astype(jnp.bfloat16)
    term = jnp.dot(shifted, head_weight, preferred_element_type=jnp.float32)
    scaled_grad = row_grad[:, None] * term * norm_gain[None, :]
    row_dot = lax.optimization_barrier(jnp.mean(hidden_f32 * scaled_grad, axis=1))
    input_grad = inv_rms[:, None] * scaled_grad - hidden_f32 * (inv_rms * inv_rms * inv_rms * row_dot)[:, None]
    hidden_grad = (LOSS_SCALE * input_grad).astype(jnp.bfloat16)
    return (loss, hidden_grad)
```

```python
import jax
import jax.numpy as jnp
from jax import lax
from jax.sharding import Mesh, PartitionSpec as P

EPSILON = 1e-05
DPO_BETA = 0.05
LOSS_SCALE = 4096.0
PLANE = ("y", "x")
CTX = ("y", "x", "c")


def spread(value, axes, count):
    return lax.all_to_all(
        jnp.broadcast_to(value[None], (count,) + value.shape), axes, 0, 0, tiled=True
    )


def other_core(value):
    return lax.ppermute(value, "c", [(0, 1), (1, 0)])


def merge_stats(stats):
    top = jnp.max(stats[:, 0], axis=0)
    total = jnp.sum(stats[:, 1] * jnp.exp(stats[:, 0] - top), axis=0)
    return jnp.stack([top, total, jnp.sum(stats[:, 2], axis=0)])


def on_device(hidden, norm_gain, head_weight, targets, ref_logprobs, block_order, lengths):
    tok_dev, part_width = hidden.shape
    voc_dev, full_width = head_weight.shape
    n_plane = lax.axis_size(PLANE)
    n_ctx = lax.axis_size(CTX)
    n_z = lax.axis_size("z")
    core = lax.axis_index("c")
    z_index = lax.axis_index("z")
    ctx_index = lax.axis_index(CTX)
    rows = tok_dev * n_ctx
    bf16, f32 = jnp.bfloat16, jnp.float32

    features = spread(hidden, "z", n_z).transpose(1, 0, 2).reshape(tok_dev, full_width)
    full_rows = features.astype(f32)
    inv_rms = lax.rsqrt(jnp.mean(full_rows * full_rows, axis=1) + EPSILON)
    normed = (full_rows * inv_rms[:, None] * norm_gain[None, :]).astype(bf16)
    own_rows = spread(normed, PLANE, n_plane).reshape(rows // 2, full_width)
    all_rows = jnp.concatenate([own_rows, other_core(own_rows)], axis=0)

    logits = lax.dot_general(
        all_rows, head_weight, (((1,), (1,)), ((), ())), preferred_element_type=f32
    )
    by_core = targets.reshape(n_plane, 2, tok_dev).transpose(1, 0, 2).reshape(2, rows // 2)
    own_first = jnp.where(core == 0, by_core, by_core[::-1]).reshape(rows)
    vocab_start = (ctx_index * n_z + z_index) * voc_dev
    columns = vocab_start + lax.broadcasted_iota(jnp.int32, (1, voc_dev), 1)
    onehot = own_first[:, None] == columns
    picked_part = jnp.sum(jnp.where(onehot, logits, 0.0), axis=1)
    local_top = jnp.max(logits, axis=1)
    local_total = jnp.sum(jnp.exp(logits - local_top[:, None]), axis=1)

    local = jnp.stack([local_top, local_total, picked_part]).reshape(3, 2, rows // 2)
    local = jnp.where(core == 0, local, local[:, ::-1]).reshape(3, rows)
    within = jnp.arange(tok_dev, dtype=jnp.int32)
    block_len = tok_dev // 4
    seq_own = within // (2 * block_len)
    half_index = within // block_len % 2
    block_start = jnp.where(half_index == 0, block_order[0], block_order[1])
    position = block_start * block_len + within % block_len
    limit = jnp.where(seq_own == 0, lengths[0], lengths[1])
    live_own = (position < limit).astype(f32)
    sign_own = 1.0 - 2.0 * seq_own.astype(f32)
    extra = jnp.concatenate([ref_logprobs, live_own * sign_own, jnp.zeros((rows - 2 * tok_dev,), f32)])
    sent = jnp.concatenate([local, extra[None]], axis=0)
    got = spread(sent, CTX, n_ctx)
    over_ctx = merge_stats(got[:, :3])
    aux = got[:, 3, : 2 * tok_dev].reshape(n_plane, 2, 2, tok_dev).transpose(2, 1, 0, 3).reshape(2, rows)
    top, row_total, picked = merge_stats(spread(over_ctx, "z", n_z))
    log_total = top + jnp.log(row_total)
    margin = jnp.sum((picked - log_total - aux[0]) * aux[1])
    loss = jax.nn.softplus(-DPO_BETA * margin)
    slope_coef = -DPO_BETA * jax.nn.sigmoid(-DPO_BETA * margin)
    row_grad = slope_coef * sign_own * live_own

    halves = log_total.reshape(2, rows // 2)
    log_total = jnp.where(core == 0, halves, halves[::-1]).reshape(rows)
    shifted = (onehot.astype(f32) - jnp.exp(logits - log_total[:, None])).astype(bf16)
    half = rows // 2
    term_other = jnp.dot(shifted[half:], head_weight, preferred_element_type=f32)
    from_other = other_core(term_other.astype(bf16))
    term_own = jnp.dot(shifted[:half], head_weight, preferred_element_type=f32)
    chip_term = (term_own + from_other.astype(f32)).astype(bf16)
    pieces = lax.all_to_all(
        chip_term.reshape(n_plane, tok_dev, full_width), PLANE, 0, 0, tiled=True
    )
    scaled = jnp.sum(pieces.astype(f32), axis=0) * norm_gain[None, :]
    dot_part = jnp.sum(full_rows * scaled, axis=1)
    last = jnp.concatenate(
        [
            scaled.reshape(tok_dev, n_z, part_width).transpose(1, 0, 2),
            jnp.broadcast_to(dot_part[None, :, None], (n_z, tok_dev, 128)),
        ],
        axis=2,
    )
    last = jnp.sum(lax.all_to_all(last, "z", 0, 0, tiled=True), axis=0)
    scaled_grad = row_grad[:, None] * last[:, :part_width]
    row_dot = row_grad * last[:, part_width] / full_width
    input_grad = (
        inv_rms[:, None] * scaled_grad
        - hidden.astype(f32) * (inv_rms * inv_rms * inv_rms * row_dot)[:, None]
    )
    return (loss, (LOSS_SCALE * input_grad).astype(bf16))


def solution(mesh):
    fine = Mesh(mesh.devices.reshape(4, 4, 2, 8), ("y", "x", "c", "z"))
    placed = (P(CTX, "z"), P(), P(CTX + ("z",), None), P(), P(CTX), P(CTX), P())
    return jax.shard_map(
        on_device, mesh=fine, in_specs=placed, out_specs=(P(), P(CTX, "z")), check_vma=False
    )
```

```python
import functools

import jax
import jax.numpy as jnp
from jax import lax
from jax.experimental import pallas as pl
from jax.experimental.pallas import tpu as pltpu
from jax.sharding import Mesh, PartitionSpec as P

EPSILON = 1e-05
DPO_BETA = 0.05
LOSS_SCALE = 4096.0
PLANE = ("y", "x")
CTX = ("y", "x", "c")
CHUNK = 2048
LANES = 128
STAT_ROWS = 8
VMEM_LIMIT = 16 * 1024 * 1024
CONTRACT_LAST = (((1,), (1,)), ((), ()))
CONTRACT_MIDDLE = (((1,), (0,)), ((), ()))
F32, BF16 = jnp.float32, jnp.bfloat16


def other_core(value):
    return lax.ppermute(value, "c", [(0, 1), (1, 0)])


def exchange(value, axes):
    return lax.all_to_all(value, axes, 0, 0, tiled=True)


IN_VMEM = pl.BlockSpec(memory_space=pltpu.VMEM)
IN_SMEM = pl.BlockSpec(memory_space=pltpu.SMEM)
IN_HBM = pl.BlockSpec(memory_space=pltpu.HBM)


def run(kernel, outputs, scratch, *operands, specs=None, flops=0, moved=0):
    return pl.pallas_call(
        kernel,
        in_specs=specs or [IN_VMEM] * len(operands),
        out_specs=[IN_VMEM] * len(outputs),
        out_shape=[pltpu.VMEM(shape, dtype) for shape, dtype in outputs],
        scratch_shapes=scratch,
        compiler_params=pltpu.CompilerParams(vmem_limit_bytes=VMEM_LIMIT),
        cost_estimate=pl.CostEstimate(flops=flops, bytes_accessed=moved, transcendentals=0),
    )(*operands)


def plane_index():
    return lax.axis_index("y") * lax.axis_size("x") + lax.axis_index("x")


def prepare_kernel(
    hidden_hbm, gain_hbm, targets_hbm, logprobs_hbm, order_hbm, lengths_hbm,
    sent_ref, hidden_out_ref, gain_out_ref, targets_out_ref, live_ref, extra_ref,
    hidden_ref, targets_ref, logprobs_ref, order_ref, lengths_ref, sems,
):
    copies = [
        pltpu.make_async_copy(source, target, sems.at[i])
        for i, (source, target) in enumerate(
            (
                (hidden_hbm, hidden_ref),
                (gain_hbm, gain_out_ref),
                (targets_hbm, targets_ref),
                (logprobs_hbm, logprobs_ref),
                (order_hbm, order_ref),
                (lengths_hbm, lengths_ref),
            )
        )
    ]
    for copy in copies:
        copy.start()
    for copy in copies:
        copy.wait()
    rows = hidden_ref.shape[0]
    core_rows = extra_ref.shape[1]
    hidden = hidden_ref[...].astype(F32)
    hidden_out_ref[...] = hidden
    twice = jnp.concatenate([hidden, hidden], axis=0).astype(sent_ref.dtype)
    for i in range(sent_ref.shape[0] // (2 * rows)):
        sent_ref[i * 2 * rows : (i + 1) * 2 * rows, :] = twice

    def live_sign(row):
        block_len = rows // 4
        rejected = row // (2 * block_len) == 1
        second = row // block_len % 2 == 1
        start = jnp.where(second, order_ref[1], order_ref[0])
        limit = jnp.where(rejected, lengths_ref[1], lengths_ref[0])
        live = start * block_len + row % block_len < limit
        return jnp.where(live, jnp.where(rejected, -1.0, 1.0), 0.0)

    live_ref[...] = live_sign(lax.broadcasted_iota(jnp.int32, live_ref.shape, 0))
    lane = lax.broadcasted_iota(jnp.int32, (1, core_rows), 1)
    mine = lane // rows == plane_index()
    logprobs = jnp.zeros((1, core_rows), F32)
    for t in range(rows):
        logprobs = jnp.where(lane % rows == t, logprobs_ref[t], logprobs)
    extra_ref[...] = jnp.zeros_like(extra_ref)
    extra_ref[3:4, :] = jnp.where(mine, logprobs, 0.0)
    extra_ref[4:5, :] = jnp.where(mine, live_sign(lane % rows), 0.0)
    count = targets_ref.shape[1]
    digit = jnp.minimum(lax.broadcasted_iota(jnp.int32, (STAT_ROWS, count), 0), 3)
    digits = lax.shift_right_logical(
        jnp.broadcast_to(targets_ref[...], (STAT_ROWS, count)), 8 * digit
    ) & 255
    source = lax.broadcasted_iota(jnp.int32, (count, core_rows), 0)
    place = lax.broadcasted_iota(jnp.int32, (count, core_rows), 1)
    wanted = (place // rows * 2 + lax.axis_index("c")) * rows + place % rows
    picked = jnp.dot(
        digits.astype(F32).astype(BF16),
        (source == wanted).astype(F32).astype(BF16),
        preferred_element_type=F32,
    )
    targets = picked[0:1] + 256.0 * picked[1:2] + 65536.0 * picked[2:3]
    targets_out_ref[...] = targets.astype(jnp.int32)


def normed_kernel(features_ref, gain_ref, out_ref, inv_ref):
    parts, rows, width = features_ref.shape
    squares = sum(
        jnp.sum(features_ref[k] * features_ref[k], axis=1, keepdims=True) for k in range(parts)
    )
    inv_rms = lax.rsqrt(squares / (parts * width) + EPSILON)
    inv_ref[...] = jnp.broadcast_to(inv_rms, inv_ref.shape)
    for k in range(parts):
        columns = slice(k * width, (k + 1) * width)
        normed = features_ref[k] * inv_rms * gain_ref[:, columns]
        twice = jnp.concatenate([normed, normed], axis=0).astype(out_ref.dtype)
        for i in range(out_ref.shape[0] // (2 * rows)):
            out_ref[i * 2 * rows : (i + 1) * 2 * rows, columns] = twice


def places_in(targets_ref, n_z, voc_dev, block):
    core = lax.axis_index("c")
    owner = core if block == 0 else 1 - core
    start = ((2 * plane_index() + owner) * n_z + lax.axis_index("z")) * voc_dev
    return targets_ref[...] - start


def is_target(places, shape):
    return lax.broadcasted_iota(jnp.int32, shape, 0) == places


def logits_kernel(
    n_z, rows_ref, own_hbm, sib_ref, targets_ref, extra_ref,
    own_logits_ref, sib_logits_ref, out_ref, own_ref, sem,
):
    copy = pltpu.make_async_copy(own_hbm, own_ref, sem)
    copy.start()
    sib_logits_ref[...] = lax.dot_general(
        sib_ref[...], rows_ref[...], CONTRACT_LAST, preferred_element_type=F32
    )
    copy.wait()
    own_logits_ref[...] = lax.dot_general(
        own_ref[...], rows_ref[...], CONTRACT_LAST, preferred_element_type=F32
    )
    parts = [own_logits_ref[...], sib_logits_ref[...]]
    top = jnp.maximum(*[jnp.max(part, axis=0, keepdims=True) for part in parts])
    total = sum(jnp.sum(jnp.exp(part - top), axis=0, keepdims=True) for part in parts)
    picked = jnp.zeros_like(top)
    for block, part in enumerate(parts):
        hot = is_target(places_in(targets_ref, n_z, part.shape[0], block), part.shape)
        picked += jnp.sum(jnp.where(hot, part, 0.0), axis=0, keepdims=True)
    for k in range(out_ref.shape[0]):
        out_ref[k, 0:1, :] = top
        out_ref[k, 1:2, :] = total
        out_ref[k, 2:3, :] = picked
        out_ref[k, 3:STAT_ROWS, :] = extra_ref[3:STAT_ROWS, :]


def merged(got_ref):
    senders = got_ref.shape[0]
    top = got_ref[0, 0:1, :]
    for k in range(1, senders):
        top = jnp.maximum(top, got_ref[k, 0:1, :])
    total, picked = jnp.zeros_like(top), jnp.zeros_like(top)
    for k in range(senders):
        total += got_ref[k, 1:2, :] * jnp.exp(got_ref[k, 0:1, :] - top)
        picked += got_ref[k, 2:3, :]
    return top, total, picked


def merge_kernel(got_ref, out_ref):
    top, total, picked = merged(got_ref)
    rest = got_ref[0, 3:STAT_ROWS, :]
    for k in range(1, got_ref.shape[0]):
        rest += got_ref[k, 3:STAT_ROWS, :]
    for k in range(out_ref.shape[0]):
        out_ref[k, 0:1, :] = top
        out_ref[k, 1:2, :] = total
        out_ref[k, 2:3, :] = picked
        out_ref[k, 3:STAT_ROWS, :] = rest


def term_kernel(
    n_z, own_logits_ref, sib_logits_ref, got_ref, targets_ref, own_ref, sib_ref,
    out_ref, part_ref, own_coef_ref, sib_coef_ref,
):
    top, total, picked = merged(got_ref)
    log_total = top + jnp.log(total)
    ratio = (picked - log_total - got_ref[0, 3:4, :]) * got_ref[0, 4:5, :]
    part_ref[...] = jnp.broadcast_to(jnp.sum(ratio, axis=1, keepdims=True), part_ref.shape)
    for block, (logits_ref, coef_ref) in enumerate(
        ((own_logits_ref, own_coef_ref), (sib_logits_ref, sib_coef_ref))
    ):
        logits = logits_ref[...]
        hot = is_target(places_in(targets_ref, n_z, logits.shape[0], block), logits.shape)
        shifted = hot.astype(F32) - jnp.exp(logits - log_total)
        coef_ref[...] = shifted.T.astype(coef_ref.dtype)

    def body(i, carry):
        columns = pl.ds(pl.multiple_of(i * CHUNK, CHUNK), CHUNK)
        out_ref[:, columns] = sum(
            lax.dot_general(
                coef_ref[...], weight_ref[:, columns], CONTRACT_MIDDLE, preferred_element_type=F32
            )
            for coef_ref, weight_ref in ((own_coef_ref, own_ref), (sib_coef_ref, sib_ref))
        ).astype(out_ref.dtype)
        return carry

    lax.fori_loop(0, out_ref.shape[1] // CHUNK, body, 0)


def reduce_kernel(pieces_ref, features_ref, gain_ref, out_ref):
    parts, rows, width = features_ref.shape
    dots = jnp.zeros((rows, 1), F32)
    for k in range(parts):
        columns = slice(k * width, (k + 1) * width)
        pairs = pieces_ref[0 : 2 * rows, columns].astype(F32)
        for i in range(1, pieces_ref.shape[0] // (2 * rows)):
            pairs += pieces_ref[i * 2 * rows : (i + 1) * 2 * rows, columns].astype(F32)
        scaled = (pairs[:rows] + pairs[rows:]) * gain_ref[:, columns]
        out_ref[k, :, :width] = scaled
        dots += jnp.sum(scaled * features_ref[k], axis=1, keepdims=True)
    lane = lax.broadcasted_iota(jnp.int32, (rows, LANES), 1)
    rest = jnp.broadcast_to(dots, (rows, LANES))
    terms = jnp.zeros((rows, LANES), F32)
    for i in range(3):
        term = rest.astype(BF16).astype(F32)
        terms = jnp.where(lane == i, term, terms)
        rest -= term
    for k in range(parts):
        out_ref[k, :, width:] = terms


def final_kernel(
    full_width, last_ref, hidden_ref, inv_ref, live_ref, own_part_ref, sib_part_ref, loss_ref, out_ref
):
    rows, width = out_ref.shape
    scaled = last_ref[0].astype(F32)
    for k in range(1, last_ref.shape[0]):
        scaled += last_ref[k].astype(F32)
    value = -DPO_BETA * (own_part_ref[...] + sib_part_ref[...])
    loss = jnp.maximum(value, 0.0) + jnp.log1p(jnp.exp(-jnp.abs(value)))
    loss_ref[...] = loss[:1, :1]
    slope = -DPO_BETA / (1.0 + jnp.exp(-value))
    row_grad = (slope * live_ref[...])[:, :1]
    inv_rms = inv_ref[:, :1]
    row_dot = row_grad * jnp.sum(scaled[:, width:], axis=1, keepdims=True) / full_width
    input_grad = inv_rms * (row_grad * scaled[:, :width]) - hidden_ref[...] * (
        inv_rms * inv_rms * inv_rms * row_dot
    )
    out_ref[...] = (LOSS_SCALE * input_grad).astype(out_ref.dtype)


def on_device(hidden, norm_gain, head_weight, targets, ref_logprobs, block_order, lengths):
    tok_dev, part_width = hidden.shape
    voc_dev, full_width = head_weight.shape
    n_plane = lax.axis_size(PLANE)
    n_z = lax.axis_size("z")
    half = tok_dev * n_plane
    rows_in_all = targets.shape[0]
    flops = 4 * half * voc_dev * full_width
    moved = 4 * (voc_dev + half) * full_width

    sib_weight = other_core(head_weight)
    sent, hidden_f32, gain, targets, live_rows, extra = run(
        prepare_kernel,
        [
            ((n_z * tok_dev, part_width), BF16),
            ((tok_dev, part_width), F32),
            ((1, full_width), F32),
            ((1, half), jnp.int32),
            ((tok_dev, LANES), F32),
            ((STAT_ROWS, half), F32),
        ],
        [
            pltpu.VMEM((tok_dev, part_width), BF16),
            pltpu.VMEM((1, rows_in_all), jnp.int32),
            pltpu.SMEM((tok_dev,), F32),
            pltpu.SMEM((2,), jnp.int32),
            pltpu.SMEM((2,), jnp.int32),
            pltpu.SemaphoreType.DMA((6,)),
        ],
        *[
            pltpu.with_memory_space_constraint(value, pltpu.HBM)
            for value in (
                hidden, norm_gain[None, :], targets[None, :], ref_logprobs, block_order, lengths
            )
        ],
        specs=[IN_HBM] * 6,
        moved=1 << 20,
    )
    sent = sent.reshape(n_z, tok_dev, part_width)

    features = exchange(sent, "z").astype(F32)
    normed, inv_rms = run(
        normed_kernel,
        [((half, full_width), BF16), ((tok_dev, LANES), F32)],
        [],
        features,
        gain,
        moved=2 * half * full_width,
    )
    normed, sib_weight = lax.optimization_barrier((normed, sib_weight))
    sib_weight = pltpu.with_memory_space_constraint(sib_weight, pltpu.VMEM)
    rows = exchange(normed.reshape(n_plane, tok_dev, full_width), PLANE)
    own_logits, sib_logits, stats, own_weight = run(
        functools.partial(logits_kernel, n_z),
        [
            ((voc_dev, half), F32),
            ((voc_dev, half), F32),
            ((n_plane, STAT_ROWS, half), F32),
            ((voc_dev, full_width), BF16),
        ],
        [pltpu.SemaphoreType.DMA],
        rows.reshape(half, full_width),
        pltpu.with_memory_space_constraint(head_weight, pltpu.HBM),
        sib_weight,
        targets,
        extra,
        specs=[IN_VMEM, IN_HBM, IN_VMEM, IN_VMEM, IN_VMEM],
        flops=flops,
        moved=moved,
    )
    (stats,) = run(
        merge_kernel, [((n_z, STAT_ROWS, half), F32)], [], exchange(stats, PLANE), moved=1 << 17
    )
    chip_term, own_part = run(
        functools.partial(term_kernel, n_z),
        [((half, full_width), BF16), ((tok_dev, LANES), F32)],
        [pltpu.VMEM((half, voc_dev), BF16)] * 2,
        own_logits,
        sib_logits,
        exchange(stats, "z"),
        targets,
        own_weight,
        sib_weight,
        flops=flops,
        moved=moved,
    )
    chip_term, sib_part = lax.optimization_barrier((chip_term, other_core(own_part)))
    pieces = exchange(chip_term.reshape(n_plane, tok_dev, full_width), PLANE)
    (last,) = run(
        reduce_kernel,
        [((n_z, tok_dev, part_width + LANES), F32)],
        [],
        pieces.reshape(half, full_width),
        features,
        gain,
        moved=4 * half * full_width,
    )
    last = exchange(last.astype(BF16), "z")
    loss, hidden_grad = pl.pallas_call(
        functools.partial(final_kernel, full_width),
        in_specs=[IN_VMEM] * 6,
        out_specs=[IN_VMEM] * 2,
        out_shape=[
            jax.ShapeDtypeStruct((1, 1), F32),
            jax.ShapeDtypeStruct((tok_dev, part_width), BF16),
        ],
        compiler_params=pltpu.CompilerParams(vmem_limit_bytes=VMEM_LIMIT),
    )(last, hidden_f32, inv_rms, live_rows, own_part, sib_part)
    return (loss[0, 0], hidden_grad)


def solution(mesh):
    fine = Mesh(mesh.devices.reshape(4, 4, 2, 8), ("y", "x", "c", "z"))
    placed = (P(CTX, "z"), P(), P(CTX + ("z",), None), P(), P(CTX), P(CTX), P())
    return jax.shard_map(
        on_device, mesh=fine, in_specs=placed, out_specs=(P(), P(CTX, "z")), check_vma=False
    )
```

```python
import functools

import jax
import jax.numpy as jnp
from jax import lax
from jax.experimental import pallas as pl
from jax.experimental.pallas import tpu as pltpu
from jax.sharding import Mesh, PartitionSpec as P

EPSILON = 1e-05
DPO_BETA = 0.05
LOSS_SCALE = 4096.0
PLANE = ("y", "x")
CTX = ("y", "x", "c")
CHUNK = 2048
LANES = 128
STAT_ROWS = 8
SIDE = 4
VMEM_LIMIT = 16 * 1024 * 1024
CONTRACT_LAST = (((1,), (1,)), ((), ()))
CONTRACT_MIDDLE = (((1,), (0,)), ((), ()))
F32, BF16 = jnp.float32, jnp.bfloat16


def other_core(value):
    return lax.ppermute(value, "c", [(0, 1), (1, 0)])


def exchange(value, axes):
    return lax.all_to_all(value, axes, 0, 0, tiled=True)


IN_VMEM = pl.BlockSpec(memory_space=pltpu.VMEM)
IN_SMEM = pl.BlockSpec(memory_space=pltpu.SMEM)
IN_HBM = pl.BlockSpec(memory_space=pltpu.HBM)


def run(kernel, outputs, scratch, *operands, specs=None, flops=0, moved=0):
    return pl.pallas_call(
        kernel,
        in_specs=specs or [IN_VMEM] * len(operands),
        out_specs=[IN_VMEM] * len(outputs),
        out_shape=[pltpu.VMEM(shape, dtype) for shape, dtype in outputs],
        scratch_shapes=scratch,
        compiler_params=pltpu.CompilerParams(vmem_limit_bytes=VMEM_LIMIT),
        cost_estimate=pl.CostEstimate(flops=flops, bytes_accessed=moved, transcendentals=0),
    )(*operands)


def plane_index():
    return lax.axis_index("y") * lax.axis_size("x") + lax.axis_index("x")


def place_on(y, x, core):
    return (jnp.where(core == 0, x, y), jnp.where(core == 0, y, x))


def own_place():
    return place_on(lax.axis_index("y"), lax.axis_index("x"), lax.axis_index("c"))


def device(y, x, core):
    return (y * SIDE + x) * 2 + core


def from_ahead(value, step, outer):
    pairs = []
    for y in range(SIDE):
        for x in range(SIDE):
            for core in range(2):
                if (core == 0) == outer:
                    source = device(y, (x + step) % SIDE, core)
                else:
                    source = device((y + step) % SIDE, x, core)
                pairs.append((source, device(y, x, core)))
    return lax.ppermute(value, CTX, pairs)


def gather_from(value, outer):
    far = from_ahead(value, 2, outer)
    return jnp.concatenate(
        [value, from_ahead(value, 1, outer), far, from_ahead(value, 3, outer)], axis=0
    )


def in_order(value, rows):
    lanes = value.shape[1]
    group = SIDE * rows
    outer, inner = own_place()
    lane = lax.broadcasted_iota(jnp.int32, value.shape, 1)
    shift = inner * rows
    ahead = pltpu.roll(value, shift, 1)
    wrapped = pltpu.roll(value, (shift + lanes - group) % lanes, 1)
    value = jnp.where(lane % group >= shift, ahead, wrapped)
    return pltpu.roll(value, outer * group, 1)


def prepare_kernel(
    hidden_hbm, gain_hbm, targets_hbm, logprobs_hbm, order_hbm, lengths_hbm,
    sent_ref, hidden_out_ref, gain_out_ref, targets_out_ref, live_ref, extra_ref,
    hidden_ref, targets_ref, logprobs_ref, order_ref, lengths_ref, sems,
):
    copies = [
        pltpu.make_async_copy(source, target, sems.at[i])
        for i, (source, target) in enumerate(
            (
                (hidden_hbm, hidden_ref),
                (gain_hbm, gain_out_ref),
                (targets_hbm, targets_ref),
                (logprobs_hbm, logprobs_ref),
                (order_hbm, order_ref),
                (lengths_hbm, lengths_ref),
            )
        )
    ]
    for copy in copies:
        copy.start()
    for copy in copies:
        copy.wait()
    rows = hidden_ref.shape[0]
    core_rows = extra_ref.shape[1]
    hidden = hidden_ref[...].astype(F32)
    hidden_out_ref[...] = hidden
    twice = jnp.concatenate([hidden, hidden], axis=0).astype(sent_ref.dtype)
    for i in range(sent_ref.shape[0] // (2 * rows)):
        sent_ref[i * 2 * rows : (i + 1) * 2 * rows, :] = twice

    def live_sign(row):
        block_len = rows // 4
        rejected = row // (2 * block_len) == 1
        second = row // block_len % 2 == 1
        start = jnp.where(second, order_ref[1], order_ref[0])
        limit = jnp.where(rejected, lengths_ref[1], lengths_ref[0])
        live = start * block_len + row % block_len < limit
        return jnp.where(live, jnp.where(rejected, -1.0, 1.0), 0.0)

    live_ref[...] = live_sign(lax.broadcasted_iota(jnp.int32, live_ref.shape, 0))
    lane = lax.broadcasted_iota(jnp.int32, (1, core_rows), 1)
    outer, inner = own_place()
    mine = lane // rows == outer * SIDE + inner
    logprobs = jnp.zeros((1, core_rows), F32)
    for t in range(rows):
        logprobs = jnp.where(lane % rows == t, logprobs_ref[t], logprobs)
    extra_ref[...] = jnp.zeros_like(extra_ref)
    extra_ref[3:4, :] = jnp.where(mine, logprobs, 0.0)
    extra_ref[4:5, :] = jnp.where(mine, live_sign(lane % rows), 0.0)
    count = targets_ref.shape[1]
    digit = jnp.minimum(lax.broadcasted_iota(jnp.int32, (STAT_ROWS, count), 0), 3)
    digits = lax.shift_right_logical(
        jnp.broadcast_to(targets_ref[...], (STAT_ROWS, count)), 8 * digit
    ) & 255
    source = lax.broadcasted_iota(jnp.int32, (count, core_rows), 0)
    place = lax.broadcasted_iota(jnp.int32, (count, core_rows), 1)
    core = lax.axis_index("c")
    x, y = place_on(place // rows % SIDE, place // (rows * SIDE), core)
    wanted = device(y, x, core) * rows + place % rows
    picked = jnp.dot(
        digits.astype(F32).astype(BF16),
        (source == wanted).astype(F32).astype(BF16),
        preferred_element_type=F32,
    )
    targets = picked[0:1] + 256.0 * picked[1:2] + 65536.0 * picked[2:3]
    targets_out_ref[...] = targets.astype(jnp.int32)


def normed_kernel(features_ref, gain_ref, out_ref, inv_ref):
    parts, rows, width = features_ref.shape
    squares = sum(
        jnp.sum(features_ref[k] * features_ref[k], axis=1, keepdims=True) for k in range(parts)
    )
    inv_rms = lax.rsqrt(squares / (parts * width) + EPSILON)
    inv_ref[...] = jnp.broadcast_to(inv_rms, inv_ref.shape)
    for k in range(parts):
        columns = slice(k * width, (k + 1) * width)
        normed = features_ref[k] * inv_rms * gain_ref[:, columns]
        out_ref[:, columns] = normed.astype(out_ref.dtype)


def places_in(targets_ref, n_z, voc_dev, block):
    core = lax.axis_index("c")
    owner = core if block == 0 else 1 - core
    start = ((2 * plane_index() + owner) * n_z + lax.axis_index("z")) * voc_dev
    return targets_ref[...] - start


def is_target(places, shape):
    return lax.broadcasted_iota(jnp.int32, shape, 0) == places


def logits_kernel(
    n_z, rows_ref, own_ref, sib_ref, targets_ref, extra_ref, own_logits_ref, sib_logits_ref, out_ref
):
    for weight_ref, logits_ref in ((own_ref, own_logits_ref), (sib_ref, sib_logits_ref)):
        logits = lax.dot_general(
            weight_ref[...], rows_ref[...], CONTRACT_LAST, preferred_element_type=F32
        )
        logits_ref[...] = in_order(logits, rows_ref.shape[0] // (SIDE * SIDE))
    parts = [own_logits_ref[...], sib_logits_ref[...]]
    top = jnp.maximum(*[jnp.max(part, axis=0, keepdims=True) for part in parts])
    total = sum(jnp.sum(jnp.exp(part - top), axis=0, keepdims=True) for part in parts)
    picked = jnp.zeros_like(top)
    for block, part in enumerate(parts):
        hot = is_target(places_in(targets_ref, n_z, part.shape[0], block), part.shape)
        picked += jnp.sum(jnp.where(hot, part, 0.0), axis=0, keepdims=True)
    for k in range(out_ref.shape[0]):
        out_ref[k, 0:1, :] = top
        out_ref[k, 1:2, :] = total
        out_ref[k, 2:3, :] = picked
        out_ref[k, 3:STAT_ROWS, :] = extra_ref[3:STAT_ROWS, :]


def merged(got_ref):
    senders = got_ref.shape[0]
    top = got_ref[0, 0:1, :]
    for k in range(1, senders):
        top = jnp.maximum(top, got_ref[k, 0:1, :])
    total, picked = jnp.zeros_like(top), jnp.zeros_like(top)
    for k in range(senders):
        total += got_ref[k, 1:2, :] * jnp.exp(got_ref[k, 0:1, :] - top)
        picked += got_ref[k, 2:3, :]
    return top, total, picked


def merge_kernel(got_ref, out_ref):
    top, total, picked = merged(got_ref)
    rest = got_ref[0, 3:STAT_ROWS, :]
    for k in range(1, got_ref.shape[0]):
        rest += got_ref[k, 3:STAT_ROWS, :]
    for k in range(out_ref.shape[0]):
        out_ref[k, 0:1, :] = top
        out_ref[k, 1:2, :] = total
        out_ref[k, 2:3, :] = picked
        out_ref[k, 3:STAT_ROWS, :] = rest


def term_kernel(
    n_z, own_logits_ref, sib_logits_ref, got_ref, targets_ref, own_ref, sib_ref,
    out_ref, part_ref, own_coef_ref, sib_coef_ref,
):
    top, total, picked = merged(got_ref)
    log_total = top + jnp.log(total)
    ratio = (picked - log_total - got_ref[0, 3:4, :]) * got_ref[0, 4:5, :]
    part_ref[...] = jnp.broadcast_to(jnp.sum(ratio, axis=1, keepdims=True), part_ref.shape)
    for block, (logits_ref, coef_ref) in enumerate(
        ((own_logits_ref, own_coef_ref), (sib_logits_ref, sib_coef_ref))
    ):
        logits = logits_ref[...]
        hot = is_target(places_in(targets_ref, n_z, logits.shape[0], block), logits.shape)
        shifted = hot.astype(F32) - jnp.exp(logits - log_total)
        coef_ref[...] = shifted.T.astype(coef_ref.dtype)

    def body(i, carry):
        columns = pl.ds(pl.multiple_of(i * CHUNK, CHUNK), CHUNK)
        out_ref[:, columns] = sum(
            lax.dot_general(
                coef_ref[...], weight_ref[:, columns], CONTRACT_MIDDLE, preferred_element_type=F32
            )
            for coef_ref, weight_ref in ((own_coef_ref, own_ref), (sib_coef_ref, sib_ref))
        ).astype(out_ref.dtype)
        return carry

    lax.fori_loop(0, out_ref.shape[1] // CHUNK, body, 0)


def reduce_kernel(pieces_ref, features_ref, gain_ref, out_ref):
    parts, rows, width = features_ref.shape
    dots = jnp.zeros((rows, 1), F32)
    for k in range(parts):
        columns = slice(k * width, (k + 1) * width)
        pairs = pieces_ref[0 : 2 * rows, columns].astype(F32)
        for i in range(1, pieces_ref.shape[0] // (2 * rows)):
            pairs += pieces_ref[i * 2 * rows : (i + 1) * 2 * rows, columns].astype(F32)
        scaled = (pairs[:rows] + pairs[rows:]) * gain_ref[:, columns]
        out_ref[k, :, :width] = scaled
        dots += jnp.sum(scaled * features_ref[k], axis=1, keepdims=True)
    for k in range(parts):
        out_ref[k, :, width:] = jnp.broadcast_to(dots, (rows, LANES))


def final_kernel(
    full_width, last_ref, hidden_ref, inv_ref, live_ref, own_part_ref, sib_part_ref, loss_ref, out_ref
):
    rows, width = out_ref.shape
    scaled = last_ref[0]
    for k in range(1, last_ref.shape[0]):
        scaled += last_ref[k]
    value = -DPO_BETA * (own_part_ref[...] + sib_part_ref[...])
    loss = jnp.maximum(value, 0.0) + jnp.log1p(jnp.exp(-jnp.abs(value)))
    loss_ref[...] = loss[:1, :1]
    slope = -DPO_BETA / (1.0 + jnp.exp(-value))
    row_grad = (slope * live_ref[...])[:, :1]
    inv_rms = inv_ref[:, :1]
    row_dot = row_grad * scaled[:, width : width + 1] / full_width
    input_grad = inv_rms * (row_grad * scaled[:, :width]) - hidden_ref[...] * (
        inv_rms * inv_rms * inv_rms * row_dot
    )
    out_ref[...] = (LOSS_SCALE * input_grad).astype(out_ref.dtype)


def on_device(hidden, norm_gain, head_weight, targets, ref_logprobs, block_order, lengths):
    tok_dev, part_width = hidden.shape
    voc_dev, full_width = head_weight.shape
    n_plane = lax.axis_size(PLANE)
    n_z = lax.axis_size("z")
    half = tok_dev * n_plane
    rows_in_all = targets.shape[0]
    flops = 4 * half * voc_dev * full_width
    moved = 4 * (voc_dev + half) * full_width

    sib_weight = other_core(head_weight)
    sent, hidden_f32, gain, targets, live_rows, extra = run(
        prepare_kernel,
        [
            ((n_z * tok_dev, part_width), BF16),
            ((tok_dev, part_width), F32),
            ((1, full_width), F32),
            ((1, half), jnp.int32),
            ((tok_dev, LANES), F32),
            ((STAT_ROWS, half), F32),
        ],
        [
            pltpu.VMEM((tok_dev, part_width), BF16),
            pltpu.VMEM((1, rows_in_all), jnp.int32),
            pltpu.SMEM((tok_dev,), F32),
            pltpu.SMEM((2,), jnp.int32),
            pltpu.SMEM((2,), jnp.int32),
            pltpu.SemaphoreType.DMA((6,)),
        ],
        *[
            pltpu.with_memory_space_constraint(value, pltpu.HBM)
            for value in (
                hidden, norm_gain[None, :], targets[None, :], ref_logprobs, block_order, lengths
            )
        ],
        specs=[IN_HBM] * 6,
        moved=1 << 20,
    )
    sent = sent.reshape(n_z, tok_dev, part_width)

    features = exchange(sent, "z").astype(F32)
    normed, inv_rms = run(
        normed_kernel,
        [((tok_dev, full_width), BF16), ((tok_dev, LANES), F32)],
        [],
        features,
        gain,
        moved=2 * half * full_width,
    )
    normed, sib_weight = lax.optimization_barrier((normed, sib_weight))
    own_weight = pltpu.with_memory_space_constraint(other_core(sib_weight), pltpu.VMEM)
    sib_weight = pltpu.with_memory_space_constraint(sib_weight, pltpu.VMEM)
    rows = gather_from(gather_from(normed, False), True)
    own_logits, sib_logits, stats = run(
        functools.partial(logits_kernel, n_z),
        [((voc_dev, half), F32), ((voc_dev, half), F32), ((n_plane, STAT_ROWS, half), F32)],
        [],
        rows,
        own_weight,
        sib_weight,
        targets,
        extra,
        flops=flops,
        moved=moved,
    )
    (stats,) = run(
        merge_kernel, [((n_z, STAT_ROWS, half), F32)], [], exchange(stats, PLANE), moved=1 << 17
    )
    chip_term, own_part = run(
        functools.partial(term_kernel, n_z),
        [((half, full_width), BF16), ((tok_dev, LANES), F32)],
        [pltpu.VMEM((half, voc_dev), BF16)] * 2,
        own_logits,
        sib_logits,
        exchange(stats, "z"),
        targets,
        own_weight,
        sib_weight,
        flops=flops,
        moved=moved,
    )
    chip_term, sib_part = lax.optimization_barrier((chip_term, other_core(own_part)))
    pieces = lax.all_to_all(
        chip_term.reshape(n_plane, tok_dev, full_width),
        CTX,
        0,
        0,
        axis_index_groups=[
            [device(y, x, 0) for x in range(SIDE) for y in range(SIDE)],
            [device(y, x, 1) for y in range(SIDE) for x in range(SIDE)],
        ],
        tiled=True,
    )
    (last,) = run(
        reduce_kernel,
        [((n_z, tok_dev, part_width + LANES), F32)],
        [],
        pieces.reshape(half, full_width),
        features,
        gain,
        moved=4 * half * full_width,
    )
    last = exchange(last, "z")
    loss, hidden_grad = pl.pallas_call(
        functools.partial(final_kernel, full_width),
        in_specs=[IN_VMEM] * 6,
        out_specs=[IN_VMEM] * 2,
        out_shape=[
            jax.ShapeDtypeStruct((1, 1), F32),
            jax.ShapeDtypeStruct((tok_dev, part_width), BF16),
        ],
        compiler_params=pltpu.CompilerParams(vmem_limit_bytes=VMEM_LIMIT),
    )(last, hidden_f32, inv_rms, live_rows, own_part, sib_part)
    return (loss[0, 0], hidden_grad)


def solution(mesh):
    fine = Mesh(mesh.devices.reshape(SIDE, SIDE, 2, 8), ("y", "x", "c", "z"))
    placed = (P(CTX, "z"), P(), P(CTX + ("z",), None), P(), P(CTX), P(CTX), P())
    return jax.shard_map(
        on_device, mesh=fine, in_specs=placed, out_specs=(P(), P(CTX, "z")), check_vma=False
    )
```

```python
import functools

import jax
import jax.numpy as jnp
from jax import lax
from jax.experimental import pallas as pl
from jax.experimental.pallas import tpu as pltpu
from jax.sharding import Mesh, PartitionSpec as P

EPSILON = 1e-05
DPO_BETA = 0.05
LOSS_SCALE = 4096.0
PLANE = ("y", "x")
CTX = ("y", "x", "c")
CHUNK = 2048
LANES = 128
STAT_ROWS = 8
SIDE = 4
VMEM_LIMIT = 16 * 1024 * 1024
CONTRACT_LAST = (((1,), (1,)), ((), ()))
CONTRACT_MIDDLE = (((1,), (0,)), ((), ()))
F32, BF16 = jnp.float32, jnp.bfloat16


def other_core(value):
    return lax.ppermute(value, "c", [(0, 1), (1, 0)])


def exchange(value, axes):
    return lax.all_to_all(value, axes, 0, 0, tiled=True)


IN_VMEM = pl.BlockSpec(memory_space=pltpu.VMEM)
IN_SMEM = pl.BlockSpec(memory_space=pltpu.SMEM)
IN_HBM = pl.BlockSpec(memory_space=pltpu.HBM)


def run(kernel, outputs, scratch, *operands, specs=None, flops=0, moved=0):
    return pl.pallas_call(
        kernel,
        in_specs=specs or [IN_VMEM] * len(operands),
        out_specs=[IN_VMEM] * len(outputs),
        out_shape=[pltpu.VMEM(shape, dtype) for shape, dtype in outputs],
        scratch_shapes=scratch,
        compiler_params=pltpu.CompilerParams(vmem_limit_bytes=VMEM_LIMIT),
        cost_estimate=pl.CostEstimate(flops=flops, bytes_accessed=moved, transcendentals=0),
    )(*operands)


def plane_index():
    return lax.axis_index("y") * lax.axis_size("x") + lax.axis_index("x")


def place_on(y, x, core):
    return (jnp.where(core == 0, x, y), jnp.where(core == 0, y, x))


def own_place():
    return place_on(lax.axis_index("y"), lax.axis_index("x"), lax.axis_index("c"))


def device(y, x, core):
    return (y * SIDE + x) * 2 + core


def from_ahead(value, step, outer):
    pairs = []
    for y in range(SIDE):
        for x in range(SIDE):
            for core in range(2):
                if (core == 0) == outer:
                    source = device(y, (x + step) % SIDE, core)
                else:
                    source = device((y + step) % SIDE, x, core)
                pairs.append((source, device(y, x, core)))
    return lax.ppermute(value, CTX, pairs)


def gather_from(value, outer):
    far = from_ahead(value, 2, outer)
    return jnp.concatenate(
        [value, from_ahead(value, 1, outer), far, from_ahead(value, 3, outer)], axis=0
    )


def by_distance(value, rows):
    lanes = value.shape[1]
    group = SIDE * rows
    outer, inner = own_place()
    value = pltpu.roll(value, (lanes - outer * group) % lanes, 1)
    lane = lax.broadcasted_iota(jnp.int32, value.shape, 1)
    shift = inner * rows
    behind = pltpu.roll(value, (lanes - shift) % lanes, 1)
    wrapped = pltpu.roll(value, (lanes - shift + group) % lanes, 1)
    return jnp.where(lane % group < group - shift, behind, wrapped)


def columns_of(row, rows):
    lanes = row.shape[1]
    return jnp.broadcast_to(row, (lanes, lanes)).T[:rows]


def in_order(value, rows):
    lanes = value.shape[1]
    group = SIDE * rows
    outer, inner = own_place()
    lane = lax.broadcasted_iota(jnp.int32, value.shape, 1)
    shift = inner * rows
    ahead = pltpu.roll(value, shift, 1)
    wrapped = pltpu.roll(value, (shift + lanes - group) % lanes, 1)
    value = jnp.where(lane % group >= shift, ahead, wrapped)
    return pltpu.roll(value, outer * group, 1)


def prepare_kernel(
    hidden_hbm, gain_hbm, targets_hbm, logprobs_hbm, order_hbm, lengths_hbm,
    sent_ref, hidden_out_ref, gain_out_ref, targets_out_ref, live_ref, extra_ref,
    hidden_ref, targets_ref, logprobs_ref, order_ref, lengths_ref, sems,
):
    copies = [
        pltpu.make_async_copy(source, target, sems.at[i])
        for i, (source, target) in enumerate(
            (
                (hidden_hbm, hidden_ref),
                (gain_hbm, gain_out_ref),
                (targets_hbm, targets_ref),
                (logprobs_hbm, logprobs_ref),
                (order_hbm, order_ref),
                (lengths_hbm, lengths_ref),
            )
        )
    ]
    for copy in copies:
        copy.start()
    for copy in copies:
        copy.wait()
    rows = hidden_ref.shape[0]
    core_rows = extra_ref.shape[1]
    hidden = hidden_ref[...].astype(F32)
    hidden_out_ref[...] = hidden
    twice = jnp.concatenate([hidden, hidden], axis=0).astype(sent_ref.dtype)
    for i in range(sent_ref.shape[0] // (2 * rows)):
        sent_ref[i * 2 * rows : (i + 1) * 2 * rows, :] = twice

    def live_sign(row):
        block_len = rows // 4
        rejected = row // (2 * block_len) == 1
        second = row // block_len % 2 == 1
        start = jnp.where(second, order_ref[1], order_ref[0])
        limit = jnp.where(rejected, lengths_ref[1], lengths_ref[0])
        live = start * block_len + row % block_len < limit
        return jnp.where(live, jnp.where(rejected, -1.0, 1.0), 0.0)

    live_ref[...] = live_sign(lax.broadcasted_iota(jnp.int32, live_ref.shape, 0))
    lane = lax.broadcasted_iota(jnp.int32, (1, core_rows), 1)
    outer, inner = own_place()
    mine = lane // rows == outer * SIDE + inner
    logprobs = jnp.zeros((1, core_rows), F32)
    for t in range(rows):
        logprobs = jnp.where(lane % rows == t, logprobs_ref[t], logprobs)
    extra_ref[...] = jnp.zeros_like(extra_ref)
    extra_ref[3:4, :] = jnp.where(mine, logprobs, 0.0)
    extra_ref[4:5, :] = jnp.where(mine, live_sign(lane % rows), 0.0)
    count = targets_ref.shape[1]
    digit = jnp.minimum(lax.broadcasted_iota(jnp.int32, (STAT_ROWS, count), 0), 3)
    digits = lax.shift_right_logical(
        jnp.broadcast_to(targets_ref[...], (STAT_ROWS, count)), 8 * digit
    ) & 255
    source = lax.broadcasted_iota(jnp.int32, (count, core_rows), 0)
    place = lax.broadcasted_iota(jnp.int32, (count, core_rows), 1)
    core = lax.axis_index("c")
    x, y = place_on(place // rows % SIDE, place // (rows * SIDE), core)
    wanted = device(y, x, core) * rows + place % rows
    picked = jnp.dot(
        digits.astype(F32).astype(BF16),
        (source == wanted).astype(F32).astype(BF16),
        preferred_element_type=F32,
    )
    targets = picked[0:1] + 256.0 * picked[1:2] + 65536.0 * picked[2:3]
    targets = by_distance(jnp.broadcast_to(targets, (STAT_ROWS, core_rows)), rows)
    targets_out_ref[...] = targets[:1].astype(jnp.int32)


def normed_kernel(features_ref, gain_ref, out_ref, inv_ref):
    parts, rows, width = features_ref.shape
    squares = sum(
        jnp.sum(features_ref[k] * features_ref[k], axis=1, keepdims=True) for k in range(parts)
    )
    inv_rms = lax.rsqrt(squares / (parts * width) + EPSILON)
    inv_ref[...] = jnp.broadcast_to(inv_rms, inv_ref.shape)
    for k in range(parts):
        columns = slice(k * width, (k + 1) * width)
        normed = features_ref[k] * inv_rms * gain_ref[:, columns]
        out_ref[:, columns] = normed.astype(out_ref.dtype)


def places_in(targets_ref, n_z, voc_dev, block):
    core = lax.axis_index("c")
    owner = core if block == 0 else 1 - core
    start = ((2 * plane_index() + owner) * n_z + lax.axis_index("z")) * voc_dev
    return targets_ref[...] - start


def is_target(places, shape):
    return lax.broadcasted_iota(jnp.int32, shape, 0) == places


def logits_kernel(
    n_z, rows_ref, own_ref, sib_ref, targets_ref, extra_ref,
    own_logits_ref, sib_logits_ref, out_ref, top_ref, own_stats_ref,
):
    for weight_ref, logits_ref in ((own_ref, own_logits_ref), (sib_ref, sib_logits_ref)):
        logits_ref[...] = lax.dot_general(
            weight_ref[...], rows_ref[...], CONTRACT_LAST, preferred_element_type=F32
        )
    parts = [own_logits_ref[...], sib_logits_ref[...]]
    top = jnp.maximum(*[jnp.max(part, axis=0, keepdims=True) for part in parts])
    total = sum(jnp.sum(jnp.exp(part - top), axis=0, keepdims=True) for part in parts)
    picked = jnp.zeros_like(top)
    for block, part in enumerate(parts):
        hot = is_target(places_in(targets_ref, n_z, part.shape[0], block), part.shape)
        picked += jnp.sum(jnp.where(hot, part, 0.0), axis=0, keepdims=True)
    top_ref[...] = jnp.broadcast_to(top, top_ref.shape)
    row = lax.broadcasted_iota(jnp.int32, top_ref.shape, 0)
    stats = jnp.where(row == 1, total, jnp.where(row == 2, picked, top))
    stats = in_order(stats, rows_ref.shape[0] // (SIDE * SIDE))
    stats = jnp.where((row == 3) | (row == 4), extra_ref[...], stats)
    own_stats_ref[...] = stats
    for k in range(out_ref.shape[0]):
        out_ref[k] = stats


def sums_kernel(
    n_z, own_logits_ref, sib_logits_ref, top_ref, targets_ref, own_ref, sib_ref,
    own_power_ref, own_hot_ref, *refs,
):
    outs, coefs = refs[: SIDE - 1], refs[SIDE - 1 :]
    rows = own_logits_ref.shape[1]
    for block, (logits_ref, coef_ref) in enumerate(zip((own_logits_ref, sib_logits_ref), coefs)):
        logits = logits_ref[...]
        hot = is_target(places_in(targets_ref, n_z, logits.shape[0], block), logits.shape)
        powers = jnp.where(hot, 0.0, jnp.exp(logits - top_ref[0:1, :]))
        coef_ref[:rows, :] = powers.T.astype(coef_ref.dtype)
        coef_ref[rows:, :] = hot.astype(F32).T.astype(coef_ref.dtype)
    size = rows // SIDE

    def body(i, carry):
        columns = pl.ds(pl.multiple_of(i * CHUNK, CHUNK), CHUNK)
        sums = sum(
            lax.dot_general(
                coef_ref[...], weight_ref[:, columns], CONTRACT_MIDDLE, preferred_element_type=F32
            )
            for coef_ref, weight_ref in zip(coefs, (own_ref, sib_ref))
        )
        own_power_ref[:, columns] = sums[:size]
        own_hot_ref[:, columns] = sums[rows : rows + size].astype(BF16)
        for k in range(1, SIDE):
            part = slice(k * size, (k + 1) * size)
            outs[k - 1][:size, columns] = sums[part].astype(BF16)
            outs[k - 1][size:, columns] = sums[rows:][part].astype(BF16)
        return carry

    lax.fori_loop(0, own_ref.shape[1] // CHUNK, body, 0)


def merged(got_ref):
    senders = got_ref.shape[0]
    top = got_ref[0, 0:1, :]
    for k in range(1, senders):
        top = jnp.maximum(top, got_ref[k, 0:1, :])
    total, picked = jnp.zeros_like(top), jnp.zeros_like(top)
    for k in range(senders):
        total += got_ref[k, 1:2, :] * jnp.exp(got_ref[k, 0:1, :] - top)
        picked += got_ref[k, 2:3, :]
    return top, total, picked


def merge_kernel(got_ref, own_ref, out_ref):
    top, total, picked = merged(got_ref)
    row = lax.broadcasted_iota(jnp.int32, own_ref.shape, 0)
    both = jnp.where(row == 0, top, jnp.where(row == 1, total, picked))
    stats = jnp.where(row < 3, both, own_ref[...])
    for k in range(out_ref.shape[0]):
        out_ref[k] = stats


def outer_kernel(got_ref, own_power_ref, own_hot_ref, *refs):
    blocks, refs = refs[: SIDE - 1], refs[SIDE - 1 :]
    power_out_ref, hot_out_ref, outs = refs[0], refs[1], refs[2 : SIDE + 1]
    factors_ref, part_ref, scale_ref = refs[SIDE + 1 :]
    size = own_power_ref.shape[0]
    rows = size // SIDE
    outer, inner = own_place()
    core = lax.axis_index("c")
    senders = got_ref.shape[0]
    plane = got_ref[0]
    entries = got_ref[0]
    for k in range(1, senders):
        plane = jnp.maximum(plane, got_ref[k])
        entries += got_ref[k]
    plane_top = plane[5:6, :]
    top, total, picked = merged(got_ref)
    log_total = top + jnp.log(total)
    ratio = (picked - log_total - entries[3:4, :]) * entries[4:5, :]
    part_ref[...] = jnp.broadcast_to(jnp.sum(ratio, axis=1, keepdims=True), part_ref.shape)
    shape = part_ref.shape
    for i, factor in enumerate((1.0 - jnp.exp(picked - log_total), jnp.exp(plane_top - log_total))):
        factor = by_distance(jnp.broadcast_to(factor, shape), rows)
        factors_ref[i] = columns_of(factor[0:1, :], rows)
    for k in range(SIDE):
        x, y = place_on(inner, (outer + SIDE - k) % SIDE, core)
        scale = jnp.exp(got_ref[y * SIDE + x] - plane_top)
        scale_ref[k] = columns_of(by_distance(scale, rows)[5:6, :], size)

    def body(i, carry):
        for j in range(CHUNK // LANES):
            columns = pl.ds(pl.multiple_of(i * CHUNK + j * LANES, LANES), LANES)
            power = scale_ref[0] * own_power_ref[:, columns]
            hot = own_hot_ref[:, columns].astype(F32)
            for k in range(1, SIDE):
                power += scale_ref[k] * blocks[k - 1][:size, columns].astype(F32)
                hot += blocks[k - 1][size:, columns].astype(F32)
            power_out_ref[:, columns] = power[:rows]
            hot_out_ref[:, columns] = hot[:rows]
            for m in range(1, SIDE):
                part = slice(m * rows, (m + 1) * rows)
                both = jnp.concatenate([power[part], hot[part]], axis=0)
                outs[m - 1][:, columns] = both.astype(BF16)
        return carry

    lax.fori_loop(0, own_power_ref.shape[1] // CHUNK, body, 0)


def reduce_kernel(factors_ref, features_ref, gain_ref, own_power_ref, own_hot_ref, *refs):
    blocks, out_ref = refs[: SIDE - 1], refs[SIDE - 1]
    parts, rows, width = features_ref.shape
    dots = jnp.zeros((rows, 1), F32)
    for k in range(parts):
        columns = slice(k * width, (k + 1) * width)
        power, hot = own_power_ref[:, columns], own_hot_ref[:, columns]
        for block in blocks:
            both = block[:, columns].astype(F32)
            power += both[:rows]
            hot += both[rows:]
        term = factors_ref[0][:, :1] * hot - factors_ref[1][:, :1] * power
        scaled = term * gain_ref[:, columns]
        out_ref[k, :, :width] = scaled
        dots += jnp.sum(scaled * features_ref[k], axis=1, keepdims=True)
    lane = lax.broadcasted_iota(jnp.int32, (rows, LANES), 1)
    rest = jnp.broadcast_to(dots, (rows, LANES))
    terms = jnp.zeros((rows, LANES), F32)
    for i in range(3):
        digits = rest.astype(BF16).astype(F32)
        terms = jnp.where(lane == i, digits, terms)
        rest -= digits
    for k in range(parts):
        out_ref[k, :, width:] = terms


def final_kernel(
    full_width, last_ref, hidden_ref, inv_ref, live_ref, own_part_ref, sib_part_ref, loss_ref, out_ref
):
    rows, width = out_ref.shape
    scaled = last_ref[0].astype(F32)
    for k in range(1, last_ref.shape[0]):
        scaled += last_ref[k].astype(F32)
    value = -DPO_BETA * (own_part_ref[...] + sib_part_ref[...])
    loss = jnp.maximum(value, 0.0) + jnp.log1p(jnp.exp(-jnp.abs(value)))
    loss_ref[...] = loss[:1, :1]
    slope = -DPO_BETA / (1.0 + jnp.exp(-value))
    row_grad = (slope * live_ref[...])[:, :1]
    inv_rms = inv_ref[:, :1]
    row_dot = row_grad * jnp.sum(scaled[:, width:], axis=1, keepdims=True) / full_width
    input_grad = inv_rms * (row_grad * scaled[:, :width]) - hidden_ref[...] * (
        inv_rms * inv_rms * inv_rms * row_dot
    )
    out_ref[...] = (LOSS_SCALE * input_grad).astype(out_ref.dtype)


def on_device(hidden, norm_gain, head_weight, targets, ref_logprobs, block_order, lengths):
    tok_dev, part_width = hidden.shape
    voc_dev, full_width = head_weight.shape
    n_plane = lax.axis_size(PLANE)
    n_z = lax.axis_size("z")
    half = tok_dev * n_plane
    rows_in_all = targets.shape[0]
    flops = 4 * half * voc_dev * full_width
    moved = 4 * (voc_dev + half) * full_width

    sib_weight = other_core(head_weight)
    sent, hidden_f32, gain, targets, live_rows, extra = run(
        prepare_kernel,
        [
            ((n_z * tok_dev, part_width), BF16),
            ((tok_dev, part_width), F32),
            ((1, full_width), F32),
            ((1, half), jnp.int32),
            ((tok_dev, LANES), F32),
            ((STAT_ROWS, half), F32),
        ],
        [
            pltpu.VMEM((tok_dev, part_width), BF16),
            pltpu.VMEM((1, rows_in_all), jnp.int32),
            pltpu.SMEM((tok_dev,), F32),
            pltpu.SMEM((2,), jnp.int32),
            pltpu.SMEM((2,), jnp.int32),
            pltpu.SemaphoreType.DMA((6,)),
        ],
        *[
            pltpu.with_memory_space_constraint(value, pltpu.HBM)
            for value in (
                hidden, norm_gain[None, :], targets[None, :], ref_logprobs, block_order, lengths
            )
        ],
        specs=[IN_HBM] * 6,
        moved=1 << 20,
    )
    sent = sent.reshape(n_z, tok_dev, part_width)

    features = exchange(sent, "z").astype(F32)
    normed, inv_rms = run(
        normed_kernel,
        [((tok_dev, full_width), BF16), ((tok_dev, LANES), F32)],
        [],
        features,
        gain,
        moved=2 * half * full_width,
    )
    normed, sib_weight = lax.optimization_barrier((normed, sib_weight))
    own_weight = other_core(sib_weight)
    sib_weight = pltpu.with_memory_space_constraint(sib_weight, pltpu.VMEM)
    rows = gather_from(gather_from(normed, False), True)
    own_weight = pltpu.with_memory_space_constraint(own_weight, pltpu.VMEM)
    block = half // SIDE
    own_logits, sib_logits, stats, tops, own_stats = run(
        functools.partial(logits_kernel, n_z),
        [
            ((voc_dev, half), F32),
            ((voc_dev, half), F32),
            ((n_z, STAT_ROWS, half), F32),
            ((STAT_ROWS, half), F32),
            ((STAT_ROWS, half), F32),
        ],
        [],
        rows,
        own_weight,
        sib_weight,
        targets,
        extra,
        flops=flops,
        moved=moved,
    )
    own_power, own_hot, *blocks = run(
        functools.partial(sums_kernel, n_z),
        [((block, full_width), F32), ((block, full_width), BF16)]
        + [((2 * block, full_width), BF16)] * (SIDE - 1),
        [pltpu.VMEM((2 * half, voc_dev), BF16)] * 2,
        own_logits,
        sib_logits,
        tops,
        targets,
        own_weight,
        sib_weight,
        flops=2 * flops,
        moved=moved,
    )
    stats, *blocks = lax.optimization_barrier((stats, *blocks))
    blocks = [from_ahead(value, SIDE - 1 - k, True) for k, value in enumerate(blocks)]
    (stats,) = run(
        merge_kernel,
        [((n_plane, STAT_ROWS, half), F32)],
        [],
        exchange(stats, "z"),
        own_stats,
        moved=1 << 17,
    )
    own_power, own_hot, *blocks, factors, own_part = run(
        outer_kernel,
        [((tok_dev, full_width), F32)] * 2
        + [((2 * tok_dev, full_width), BF16)] * (SIDE - 1)
        + [((2, tok_dev, half), F32), ((tok_dev, LANES), F32)],
        [pltpu.VMEM((SIDE, block, half), F32)],
        exchange(stats, PLANE),
        own_power,
        own_hot,
        *blocks,
        moved=8 * half * full_width,
    )
    blocks = [from_ahead(value, SIDE - 1 - k, False) for k, value in enumerate(blocks)]
    sib_part = other_core(own_part)
    (last,) = run(
        reduce_kernel,
        [((n_z, tok_dev, part_width + LANES), F32)],
        [],
        factors,
        features,
        gain,
        own_power,
        own_hot,
        *blocks,
        moved=4 * half * full_width,
    )
    last, sib_part = lax.optimization_barrier((last, sib_part))
    last = exchange(last.astype(BF16), "z")
    loss, hidden_grad = pl.pallas_call(
        functools.partial(final_kernel, full_width),
        in_specs=[IN_VMEM] * 6,
        out_specs=[IN_VMEM] * 2,
        out_shape=[
            jax.ShapeDtypeStruct((1, 1), F32),
            jax.ShapeDtypeStruct((tok_dev, part_width), BF16),
        ],
        compiler_params=pltpu.CompilerParams(vmem_limit_bytes=VMEM_LIMIT),
    )(last, hidden_f32, inv_rms, live_rows, own_part, sib_part)
    return (loss[0, 0], hidden_grad)


def solution(mesh):
    fine = Mesh(mesh.devices.reshape(SIDE, SIDE, 2, 8), ("y", "x", "c", "z"))
    placed = (P(CTX, "z"), P(), P(CTX + ("z",), None), P(), P(CTX), P(CTX), P())
    return jax.shard_map(
        on_device, mesh=fine, in_specs=placed, out_specs=(P(), P(CTX, "z")), check_vma=False
    )
```

```python
import functools

import jax
import jax.numpy as jnp
from jax import lax
from jax.experimental import pallas as pl
from jax.experimental.pallas import tpu as pltpu
from jax.sharding import Mesh, PartitionSpec as P

EPSILON = 1e-05
DPO_BETA = 0.05
LOSS_SCALE = 4096.0
PLANE = ("y", "x")
CTX = ("y", "x", "c")
CHUNK = 2048
LANES = 128
STAT_ROWS = 8
SIDE = 4
VMEM_LIMIT = 16 * 1024 * 1024
CONTRACT_LAST = (((1,), (1,)), ((), ()))
CONTRACT_MIDDLE = (((1,), (0,)), ((), ()))
F32, BF16 = jnp.float32, jnp.bfloat16


def other_core(value):
    return lax.ppermute(value, "c", [(0, 1), (1, 0)])


def exchange(value, axes):
    return lax.all_to_all(value, axes, 0, 0, tiled=True)


IN_VMEM = pl.BlockSpec(memory_space=pltpu.VMEM)
IN_SMEM = pl.BlockSpec(memory_space=pltpu.SMEM)
IN_HBM = pl.BlockSpec(memory_space=pltpu.HBM)


def run(kernel, outputs, scratch, *operands, specs=None, flops=0, moved=0):
    return pl.pallas_call(
        kernel,
        in_specs=specs or [IN_VMEM] * len(operands),
        out_specs=[IN_VMEM] * len(outputs),
        out_shape=[pltpu.VMEM(shape, dtype) for shape, dtype in outputs],
        scratch_shapes=scratch,
        compiler_params=pltpu.CompilerParams(vmem_limit_bytes=VMEM_LIMIT),
        cost_estimate=pl.CostEstimate(flops=flops, bytes_accessed=moved, transcendentals=0),
    )(*operands)


def plane_index():
    return lax.axis_index("y") * lax.axis_size("x") + lax.axis_index("x")


def place_on(y, x, core):
    return (jnp.where(core == 0, x, y), jnp.where(core == 0, y, x))


def own_place():
    return place_on(lax.axis_index("y"), lax.axis_index("x"), lax.axis_index("c"))


def device(y, x, core):
    return (y * SIDE + x) * 2 + core


def from_ahead(value, step, outer):
    pairs = []
    for y in range(SIDE):
        for x in range(SIDE):
            for core in range(2):
                if (core == 0) == outer:
                    source = device(y, (x + step) % SIDE, core)
                else:
                    source = device((y + step) % SIDE, x, core)
                pairs.append((source, device(y, x, core)))
    return lax.ppermute(value, CTX, pairs)


def gather_from(value, outer):
    far = from_ahead(value, 2, outer)
    return jnp.concatenate(
        [value, from_ahead(value, 1, outer), far, from_ahead(value, 3, outer)], axis=0
    )


def by_distance(value, rows):
    lanes = value.shape[1]
    group = SIDE * rows
    outer, inner = own_place()
    value = pltpu.roll(value, (lanes - outer * group) % lanes, 1)
    lane = lax.broadcasted_iota(jnp.int32, value.shape, 1)
    shift = inner * rows
    behind = pltpu.roll(value, (lanes - shift) % lanes, 1)
    wrapped = pltpu.roll(value, (lanes - shift + group) % lanes, 1)
    return jnp.where(lane % group < group - shift, behind, wrapped)


def columns_of(row, rows):
    lanes = row.shape[1]
    return jnp.broadcast_to(row, (lanes, lanes)).T[:rows]


def in_order(value, rows):
    lanes = value.shape[1]
    group = SIDE * rows
    outer, inner = own_place()
    lane = lax.broadcasted_iota(jnp.int32, value.shape, 1)
    shift = inner * rows
    ahead = pltpu.roll(value, shift, 1)
    wrapped = pltpu.roll(value, (shift + lanes - group) % lanes, 1)
    value = jnp.where(lane % group >= shift, ahead, wrapped)
    return pltpu.roll(value, outer * group, 1)


def prepare_kernel(
    hidden_hbm, gain_hbm, targets_hbm, logprobs_hbm, order_hbm, lengths_hbm,
    sent_ref, hidden_out_ref, gain_out_ref, targets_out_ref, live_ref, extra_ref,
    hidden_ref, targets_ref, logprobs_ref, order_ref, lengths_ref, sems,
):
    copies = [
        pltpu.make_async_copy(source, target, sems.at[i])
        for i, (source, target) in enumerate(
            (
                (hidden_hbm, hidden_ref),
                (gain_hbm, gain_out_ref),
                (targets_hbm, targets_ref),
                (logprobs_hbm, logprobs_ref),
                (order_hbm, order_ref),
                (lengths_hbm, lengths_ref),
            )
        )
    ]
    for copy in copies:
        copy.start()
    for copy in copies:
        copy.wait()
    rows = hidden_ref.shape[0]
    core_rows = extra_ref.shape[1]
    hidden = hidden_ref[...].astype(F32)
    hidden_out_ref[...] = hidden
    twice = jnp.concatenate([hidden, hidden], axis=0).astype(sent_ref.dtype)
    for i in range(sent_ref.shape[0] // (2 * rows)):
        sent_ref[i * 2 * rows : (i + 1) * 2 * rows, :] = twice

    def live_sign(row):
        block_len = rows // 4
        rejected = row // (2 * block_len) == 1
        second = row // block_len % 2 == 1
        start = jnp.where(second, order_ref[1], order_ref[0])
        limit = jnp.where(rejected, lengths_ref[1], lengths_ref[0])
        live = start * block_len + row % block_len < limit
        return jnp.where(live, jnp.where(rejected, -1.0, 1.0), 0.0)

    live_ref[...] = live_sign(lax.broadcasted_iota(jnp.int32, live_ref.shape, 0))
    lane = lax.broadcasted_iota(jnp.int32, (1, core_rows), 1)
    outer, inner = own_place()
    mine = lane // rows == outer * SIDE + inner
    logprobs = jnp.zeros((1, core_rows), F32)
    for t in range(rows):
        logprobs = jnp.where(lane % rows == t, logprobs_ref[t], logprobs)
    extra_ref[...] = jnp.zeros_like(extra_ref)
    extra_ref[3:4, :] = jnp.where(mine, logprobs, 0.0)
    extra_ref[4:5, :] = jnp.where(mine, live_sign(lane % rows), 0.0)
    count = targets_ref.shape[1]
    digit = jnp.minimum(lax.broadcasted_iota(jnp.int32, (STAT_ROWS, count), 0), 3)
    digits = lax.shift_right_logical(
        jnp.broadcast_to(targets_ref[...], (STAT_ROWS, count)), 8 * digit
    ) & 255
    source = lax.broadcasted_iota(jnp.int32, (count, core_rows), 0)
    place = lax.broadcasted_iota(jnp.int32, (count, core_rows), 1)
    core = lax.axis_index("c")
    x, y = place_on(place // rows % SIDE, place // (rows * SIDE), core)
    wanted = device(y, x, core) * rows + place % rows
    picked = jnp.dot(
        digits.astype(F32).astype(BF16),
        (source == wanted).astype(F32).astype(BF16),
        preferred_element_type=F32,
    )
    targets = picked[0:1] + 256.0 * picked[1:2] + 65536.0 * picked[2:3]
    targets = by_distance(jnp.broadcast_to(targets, (STAT_ROWS, core_rows)), rows)
    targets_out_ref[...] = targets[:1].astype(jnp.int32)


def normed_kernel(features_ref, gain_ref, out_ref, inv_ref):
    parts, rows, width = features_ref.shape
    squares = sum(
        jnp.sum(features_ref[k] * features_ref[k], axis=1, keepdims=True) for k in range(parts)
    )
    inv_rms = lax.rsqrt(squares / (parts * width) + EPSILON)
    inv_ref[...] = jnp.broadcast_to(inv_rms, inv_ref.shape)
    for k in range(parts):
        columns = slice(k * width, (k + 1) * width)
        normed = features_ref[k] * inv_rms * gain_ref[:, columns]
        out_ref[:, columns] = normed.astype(out_ref.dtype)


def places_in(targets_ref, n_z, voc_dev, block):
    core = lax.axis_index("c")
    owner = core if block == 0 else 1 - core
    start = ((2 * plane_index() + owner) * n_z + lax.axis_index("z")) * voc_dev
    return targets_ref[...] - start


def is_target(places, shape):
    return lax.broadcasted_iota(jnp.int32, shape, 0) == places


def first_logits_kernel(rows_ref, own_ref, sib_ref, own_logits_ref, sib_logits_ref):
    width = rows_ref.shape[1]
    for weight_ref, logits_ref in ((own_ref, own_logits_ref), (sib_ref, sib_logits_ref)):
        logits_ref[...] = lax.dot_general(
            weight_ref[:, :width], rows_ref[...], CONTRACT_LAST, preferred_element_type=F32
        )


def logits_kernel(
    n_z, rows_ref, own_first_ref, sib_first_ref, own_ref, sib_ref, targets_ref, extra_ref,
    own_logits_ref, sib_logits_ref, out_ref, top_ref, own_stats_ref,
):
    width = rows_ref.shape[1]
    for weight_ref, first_ref, logits_ref in (
        (own_ref, own_first_ref, own_logits_ref),
        (sib_ref, sib_first_ref, sib_logits_ref),
    ):
        logits_ref[...] = first_ref[...] + lax.dot_general(
            weight_ref[:, width:], rows_ref[...], CONTRACT_LAST, preferred_element_type=F32
        )
    parts = [own_logits_ref[...], sib_logits_ref[...]]
    top = jnp.maximum(*[jnp.max(part, axis=0, keepdims=True) for part in parts])
    total = sum(jnp.sum(jnp.exp(part - top), axis=0, keepdims=True) for part in parts)
    weighted = sum(jnp.sum(jnp.exp(part - top) * part, axis=0, keepdims=True) for part in parts)
    picked = jnp.zeros_like(top)
    for block, part in enumerate(parts):
        hot = is_target(places_in(targets_ref, n_z, part.shape[0], block), part.shape)
        picked += jnp.sum(jnp.where(hot, part, 0.0), axis=0, keepdims=True)
    top_ref[...] = jnp.broadcast_to(top, top_ref.shape)
    row = lax.broadcasted_iota(jnp.int32, top_ref.shape, 0)
    stats = jnp.where(row == 1, total, jnp.where(row == 2, picked, top))
    stats = jnp.where(row == 6, weighted, stats)
    stats = in_order(stats, rows_ref.shape[0] // (SIDE * SIDE))
    stats = jnp.where((row == 3) | (row == 4), extra_ref[...], stats)
    own_stats_ref[...] = stats
    for k in range(out_ref.shape[0]):
        out_ref[k] = stats


def sums_kernel(
    n_z, own_logits_ref, sib_logits_ref, top_ref, targets_ref, own_ref, sib_ref,
    ahead_ref, behind_ref, own_rest_ref, sib_rest_ref, *coefs,
):
    rows = own_logits_ref.shape[1]
    size = rows // SIDE
    rests = (own_rest_ref, sib_rest_ref)
    for block, (logits_ref, coef_ref) in enumerate(zip((own_logits_ref, sib_logits_ref), coefs)):
        logits = logits_ref[...]
        hot = is_target(places_in(targets_ref, n_z, logits.shape[0], block), logits.shape)
        powers = jnp.where(hot, 0.0, jnp.exp(logits - top_ref[0:1, :])).T
        hot = hot.astype(F32).T
        for k in range(SIDE):
            target_ref = (rests[block], coef_ref)[k % 2]
            start = k // 2 * 2 * size
            part = slice(k * size, (k + 1) * size)
            target_ref[start : start + size, :] = powers[part].astype(BF16)
            target_ref[start + size : start + 2 * size, :] = hot[part].astype(BF16)
    sums = products(coefs, (own_ref, sib_ref))
    ahead_ref[...] = sums[: 2 * size].astype(BF16)
    behind_ref[...] = sums[2 * size :].astype(BF16)


def products(coefs, weights):
    return sum(
        lax.dot_general(
            coef_ref[...], weight_ref[...], CONTRACT_MIDDLE, preferred_element_type=F32
        )
        for coef_ref, weight_ref in zip(coefs, weights)
    )


def rest_kernel(own_rest_ref, sib_rest_ref, own_ref, sib_ref, own_power_ref, own_hot_ref, far_ref):
    size = own_power_ref.shape[0]
    sums = products((own_rest_ref, sib_rest_ref), (own_ref, sib_ref))
    own_power_ref[...] = sums[:size]
    own_hot_ref[...] = sums[size : 2 * size].astype(BF16)
    far_ref[...] = sums[2 * size :].astype(BF16)


def merged(got_ref):
    senders = got_ref.shape[0]
    top = got_ref[0, 0:1, :]
    for k in range(1, senders):
        top = jnp.maximum(top, got_ref[k, 0:1, :])
    total, picked, weighted = [jnp.zeros_like(top)] * 3
    for k in range(senders):
        scale = jnp.exp(got_ref[k, 0:1, :] - top)
        total += got_ref[k, 1:2, :] * scale
        weighted += got_ref[k, 6:7, :] * scale
        picked += got_ref[k, 2:3, :]
    return top, total, picked, weighted


def merge_kernel(got_ref, own_ref, out_ref):
    top, total, picked, weighted = merged(got_ref)
    row = lax.broadcasted_iota(jnp.int32, own_ref.shape, 0)
    stats = own_ref[...]
    for i, value in ((0, top), (1, total), (2, picked), (6, weighted)):
        stats = jnp.where(row == i, value, stats)
    for k in range(out_ref.shape[0]):
        out_ref[k] = stats


def totals_kernel(got_ref, part_ref, dots_ref):
    rows, lanes = part_ref.shape
    top, total, picked, weighted = merged(got_ref)
    entries = got_ref[0]
    for k in range(1, got_ref.shape[0]):
        entries += got_ref[k]
    log_total = top + jnp.log(total)
    ratio = (picked - log_total - entries[3:4, :]) * entries[4:5, :]
    part_ref[...] = jnp.broadcast_to(jnp.sum(ratio, axis=1, keepdims=True), part_ref.shape)
    dots = jnp.broadcast_to(picked - weighted / total, (STAT_ROWS, lanes))
    dots_ref[...] = columns_of(by_distance(dots, rows)[0:1, :], rows)


def outer_kernel(got_ref, own_power_ref, own_hot_ref, *refs):
    blocks, (out_ref, scale_ref, total_ref) = refs[: SIDE - 1], refs[SIDE - 1 :]
    size = own_power_ref.shape[0]
    rows = size // SIDE
    parts = out_ref.shape[0] // SIDE
    width = out_ref.shape[2]
    outer, inner = own_place()
    core = lax.axis_index("c")
    top, total, picked, _ = merged(got_ref)
    log_total = top + jnp.log(total)
    shape = got_ref.shape[1:]
    hot_factor = by_distance(jnp.broadcast_to(1.0 - jnp.exp(picked - log_total), shape), rows)
    scale_ref[SIDE] = columns_of(hot_factor[0:1, :], size)
    for k in range(SIDE):
        x, y = place_on(inner, (outer + SIDE - k) % SIDE, core)
        scale = jnp.exp(got_ref[y * SIDE + x] - log_total)
        scale_ref[k] = columns_of(by_distance(scale, rows)[5:6, :], size)
    for z in range(parts):
        for j in range(width // LANES):
            columns = slice(z * width + j * LANES, z * width + (j + 1) * LANES)
            power = scale_ref[0] * own_power_ref[:, columns]
            hot = own_hot_ref[:, columns].astype(F32)
            for k in range(1, SIDE):
                power += scale_ref[k] * blocks[k - 1][:size, columns].astype(F32)
                hot += blocks[k - 1][size:, columns].astype(F32)
            total_ref[:, j * LANES : (j + 1) * LANES] = scale_ref[SIDE] * hot - power
        for m in range(SIDE):
            term = total_ref[m * rows : (m + 1) * rows, :]
            out_ref[(inner + m) % SIDE * parts + z] = term.astype(out_ref.dtype)


def final_kernel(
    full_width, last_ref, hidden_ref, gain_ref, inv_ref, live_ref, dots_ref, own_part_ref,
    sib_part_ref, loss_ref, out_ref,
):
    rows, width = out_ref.shape
    term = last_ref[0].astype(F32)
    for k in range(1, last_ref.shape[0]):
        term += last_ref[k].astype(F32)
    own = pl.ds(pl.multiple_of(lax.axis_index("z") * width, width), width)
    value = -DPO_BETA * (own_part_ref[...] + sib_part_ref[...])
    loss = jnp.maximum(value, 0.0) + jnp.log1p(jnp.exp(-jnp.abs(value)))
    loss_ref[...] = loss[:1, :1]
    slope = -DPO_BETA / (1.0 + jnp.exp(-value))
    row_grad = (slope * live_ref[...])[:, :1]
    inv_rms = inv_ref[:, :1]
    row_dot = row_grad * (dots_ref[:, :1] / inv_rms) / full_width
    input_grad = inv_rms * (row_grad * (term * gain_ref[:, own])) - hidden_ref[...] * (
        inv_rms * inv_rms * inv_rms * row_dot
    )
    out_ref[...] = (LOSS_SCALE * input_grad).astype(out_ref.dtype)


def along_inner_and_z(value, n_z):
    groups = [
        [
            device(*((inner, outer) if core == 0 else (outer, inner)), core) * n_z + z
            for inner in range(SIDE)
            for z in range(n_z)
        ]
        for core in range(2)
        for outer in range(SIDE)
    ]
    return lax.all_to_all(
        value, CTX + ("z",), 0, 0, axis_index_groups=groups, tiled=True
    )


def on_device(hidden, norm_gain, head_weight, targets, ref_logprobs, block_order, lengths):
    tok_dev, part_width = hidden.shape
    voc_dev, full_width = head_weight.shape
    n_plane = lax.axis_size(PLANE)
    n_z = lax.axis_size("z")
    half = tok_dev * n_plane
    rows_in_all = targets.shape[0]
    flops = 4 * half * voc_dev * full_width
    moved = 4 * (voc_dev + half) * full_width

    sib_weight = other_core(head_weight)
    sent, hidden_f32, gain, targets, live_rows, extra = run(
        prepare_kernel,
        [
            ((n_z * tok_dev, part_width), BF16),
            ((tok_dev, part_width), F32),
            ((1, full_width), F32),
            ((1, half), jnp.int32),
            ((tok_dev, LANES), F32),
            ((STAT_ROWS, half), F32),
        ],
        [
            pltpu.VMEM((tok_dev, part_width), BF16),
            pltpu.VMEM((1, rows_in_all), jnp.int32),
            pltpu.SMEM((tok_dev,), F32),
            pltpu.SMEM((2,), jnp.int32),
            pltpu.SMEM((2,), jnp.int32),
            pltpu.SemaphoreType.DMA((6,)),
        ],
        *[
            pltpu.with_memory_space_constraint(value, pltpu.HBM)
            for value in (
                hidden, norm_gain[None, :], targets[None, :], ref_logprobs, block_order, lengths
            )
        ],
        specs=[IN_HBM] * 6,
        moved=1 << 20,
    )
    sent = sent.reshape(n_z, tok_dev, part_width)

    features = exchange(sent, "z").astype(F32)
    normed, inv_rms = run(
        normed_kernel,
        [((tok_dev, full_width), BF16), ((tok_dev, LANES), F32)],
        [],
        features,
        gain,
        moved=2 * half * full_width,
    )
    normed, sib_weight = lax.optimization_barrier((normed, sib_weight))
    own_weight = other_core(sib_weight)
    sib_weight = pltpu.with_memory_space_constraint(sib_weight, pltpu.VMEM)
    nearby = gather_from(normed, False)
    first = gather_from(nearby[:, : full_width // 2], True)
    rows = gather_from(nearby[:, full_width // 2 :], True)
    own_weight = pltpu.with_memory_space_constraint(own_weight, pltpu.VMEM)
    block = half // SIDE
    first_logits = run(
        first_logits_kernel,
        [((voc_dev, half), F32)] * 2,
        [],
        first,
        own_weight,
        sib_weight,
        flops=flops // 2,
        moved=moved // 2,
    )
    own_logits, sib_logits, stats, tops, own_stats = run(
        functools.partial(logits_kernel, n_z),
        [
            ((voc_dev, half), F32),
            ((voc_dev, half), F32),
            ((n_z, STAT_ROWS, half), F32),
            ((STAT_ROWS, half), F32),
            ((STAT_ROWS, half), F32),
        ],
        [],
        rows,
        *first_logits,
        own_weight,
        sib_weight,
        targets,
        extra,
        flops=flops,
        moved=moved,
    )
    ahead, behind, own_rest, sib_rest = run(
        functools.partial(sums_kernel, n_z),
        [((2 * block, full_width), BF16)] * 2 + [((half, voc_dev), BF16)] * 2,
        [pltpu.VMEM((half, voc_dev), BF16)] * 2,
        own_logits,
        sib_logits,
        tops,
        targets,
        own_weight,
        sib_weight,
        flops=flops,
        moved=moved,
    )
    ahead, behind = from_ahead(ahead, 3, True), from_ahead(behind, 1, True)
    own_power, own_hot, far = run(
        rest_kernel,
        [
            ((block, full_width), F32),
            ((block, full_width), BF16),
            ((2 * block, full_width), BF16),
        ],
        [],
        own_rest,
        sib_rest,
        own_weight,
        sib_weight,
        flops=flops,
        moved=moved,
    )
    stats, far = lax.optimization_barrier((stats, far))
    blocks = [ahead, from_ahead(far, 2, True), behind]
    (stats,) = run(
        merge_kernel,
        [((n_plane, STAT_ROWS, half), F32)],
        [],
        exchange(stats, "z"),
        own_stats,
        moved=1 << 17,
    )
    got = exchange(stats, PLANE)
    own_part, dots = run(
        totals_kernel, [((tok_dev, LANES), F32)] * 2, [], got, moved=1 << 17
    )
    sib_part = other_core(own_part)
    (last,) = run(
        outer_kernel,
        [((SIDE * n_z, tok_dev, part_width), BF16)],
        [pltpu.VMEM((SIDE + 1, block, half), F32), pltpu.VMEM((block, part_width), F32)],
        got,
        own_power,
        own_hot,
        *blocks,
        moved=8 * half * full_width,
    )
    last, sib_part = lax.optimization_barrier((last, sib_part))
    last = along_inner_and_z(last, n_z)
    loss, hidden_grad = pl.pallas_call(
        functools.partial(final_kernel, full_width),
        in_specs=[IN_VMEM] * 8,
        out_specs=[IN_VMEM] * 2,
        out_shape=[
            jax.ShapeDtypeStruct((1, 1), F32),
            jax.ShapeDtypeStruct((tok_dev, part_width), BF16),
        ],
        compiler_params=pltpu.CompilerParams(vmem_limit_bytes=VMEM_LIMIT),
    )(last, hidden_f32, gain, inv_rms, live_rows, dots, own_part, sib_part)
    return (loss[0, 0], hidden_grad)


def solution(mesh):
    fine = Mesh(mesh.devices.reshape(SIDE, SIDE, 2, 8), ("y", "x", "c", "z"))
    placed = (P(CTX, "z"), P(), P(CTX + ("z",), None), P(), P(CTX), P(CTX), P())
    return jax.shard_map(
        on_device, mesh=fine, in_specs=placed, out_specs=(P(), P(CTX, "z")), check_vma=False
    )
```

```python
import functools

import jax
import jax.numpy as jnp
from jax import lax
from jax.experimental import pallas as pl
from jax.experimental.pallas import tpu as pltpu
from jax.sharding import Mesh, PartitionSpec as P

EPSILON = 1e-05
DPO_BETA = 0.05
LOSS_SCALE = 4096.0
PLANE = ("y", "x")
CTX = ("y", "x", "c")
CHUNK = 2048
LANES = 128
STAT_ROWS = 8
SIDE = 4
VMEM_LIMIT = 16 * 1024 * 1024
CONTRACT_LAST = (((1,), (1,)), ((), ()))
CONTRACT_MIDDLE = (((1,), (0,)), ((), ()))
F32, BF16 = jnp.float32, jnp.bfloat16


def other_core(value):
    return lax.ppermute(value, "c", [(0, 1), (1, 0)])


def exchange(value, axes):
    return lax.all_to_all(value, axes, 0, 0, tiled=True)


IN_VMEM = pl.BlockSpec(memory_space=pltpu.VMEM)
IN_SMEM = pl.BlockSpec(memory_space=pltpu.SMEM)
IN_HBM = pl.BlockSpec(memory_space=pltpu.HBM)


def run(kernel, outputs, scratch, *operands, specs=None, flops=0, moved=0):
    return pl.pallas_call(
        kernel,
        in_specs=specs or [IN_VMEM] * len(operands),
        out_specs=[IN_VMEM] * len(outputs),
        out_shape=[pltpu.VMEM(shape, dtype) for shape, dtype in outputs],
        scratch_shapes=scratch,
        compiler_params=pltpu.CompilerParams(vmem_limit_bytes=VMEM_LIMIT),
        cost_estimate=pl.CostEstimate(flops=flops, bytes_accessed=moved, transcendentals=0),
    )(*operands)


def plane_index():
    return lax.axis_index("y") * lax.axis_size("x") + lax.axis_index("x")


def own_group():
    return (lax.axis_index("c") + lax.axis_index("x") + lax.axis_index("y")) % 2


def place_on(y, x, group):
    return (jnp.where(group == 0, x, y), jnp.where(group == 0, y, x))


def own_place():
    return place_on(lax.axis_index("y"), lax.axis_index("x"), own_group())


def device(y, x, group):
    return (y * SIDE + x) * 2 + (group + x + y) % 2


def from_ahead(value, step, outer):
    pairs = []
    for y in range(SIDE):
        for x in range(SIDE):
            for core in range(2):
                if (core == 0) == outer:
                    source = device(y, (x + step) % SIDE, core)
                else:
                    source = device((y + step) % SIDE, x, core)
                pairs.append((source, device(y, x, core)))
    return lax.ppermute(value, CTX, pairs)


def gather_from(value, outer):
    far = from_ahead(value, 2, outer)
    return jnp.concatenate(
        [value, from_ahead(value, 1, outer), far, from_ahead(value, 3, outer)], axis=0
    )


def by_distance(value, rows):
    lanes = value.shape[1]
    group = SIDE * rows
    outer, inner = own_place()
    value = pltpu.roll(value, (lanes - outer * group) % lanes, 1)
    lane = lax.broadcasted_iota(jnp.int32, value.shape, 1)
    shift = inner * rows
    behind = pltpu.roll(value, (lanes - shift) % lanes, 1)
    wrapped = pltpu.roll(value, (lanes - shift + group) % lanes, 1)
    return jnp.where(lane % group < group - shift, behind, wrapped)


def columns_of(row, rows):
    lanes = row.shape[1]
    return jnp.broadcast_to(row, (lanes, lanes)).T[:rows]


def in_order(value, rows):
    lanes = value.shape[1]
    group = SIDE * rows
    outer, inner = own_place()
    lane = lax.broadcasted_iota(jnp.int32, value.shape, 1)
    shift = inner * rows
    ahead = pltpu.roll(value, shift, 1)
    wrapped = pltpu.roll(value, (shift + lanes - group) % lanes, 1)
    value = jnp.where(lane % group >= shift, ahead, wrapped)
    return pltpu.roll(value, outer * group, 1)


def prepare_kernel(
    hidden_hbm, gain_hbm, targets_hbm, logprobs_hbm, order_hbm, lengths_hbm,
    sent_ref, hidden_out_ref, gain_out_ref, targets_out_ref, live_ref, extra_ref,
    hidden_ref, targets_ref, logprobs_ref, order_ref, lengths_ref, sems,
):
    copies = [
        pltpu.make_async_copy(source, target, sems.at[i])
        for i, (source, target) in enumerate(
            (
                (hidden_hbm, hidden_ref),
                (gain_hbm, gain_out_ref),
                (targets_hbm, targets_ref),
                (logprobs_hbm, logprobs_ref),
                (order_hbm, order_ref),
                (lengths_hbm, lengths_ref),
            )
        )
    ]
    for copy in copies:
        copy.start()
    for copy in copies:
        copy.wait()
    rows = hidden_ref.shape[0]
    core_rows = extra_ref.shape[1]
    hidden = hidden_ref[...].astype(F32)
    hidden_out_ref[...] = hidden
    twice = jnp.concatenate([hidden, hidden], axis=0).astype(sent_ref.dtype)
    for i in range(sent_ref.shape[0] // (2 * rows)):
        sent_ref[i * 2 * rows : (i + 1) * 2 * rows, :] = twice

    def live_sign(row):
        block_len = rows // 4
        rejected = row // (2 * block_len) == 1
        second = row // block_len % 2 == 1
        start = jnp.where(second, order_ref[1], order_ref[0])
        limit = jnp.where(rejected, lengths_ref[1], lengths_ref[0])
        live = start * block_len + row % block_len < limit
        return jnp.where(live, jnp.where(rejected, -1.0, 1.0), 0.0)

    live_ref[...] = live_sign(lax.broadcasted_iota(jnp.int32, live_ref.shape, 0))
    lane = lax.broadcasted_iota(jnp.int32, (1, core_rows), 1)
    outer, inner = own_place()
    mine = lane // rows == outer * SIDE + inner
    logprobs = jnp.zeros((1, core_rows), F32)
    for t in range(rows):
        logprobs = jnp.where(lane % rows == t, logprobs_ref[t], logprobs)
    extra_ref[...] = jnp.zeros_like(extra_ref)
    extra_ref[3:4, :] = jnp.where(mine, logprobs, 0.0)
    extra_ref[4:5, :] = jnp.where(mine, live_sign(lane % rows), 0.0)
    count = targets_ref.shape[1]
    digit = jnp.minimum(lax.broadcasted_iota(jnp.int32, (STAT_ROWS, count), 0), 3)
    digits = lax.shift_right_logical(
        jnp.broadcast_to(targets_ref[...], (STAT_ROWS, count)), 8 * digit
    ) & 255
    source = lax.broadcasted_iota(jnp.int32, (count, core_rows), 0)
    place = lax.broadcasted_iota(jnp.int32, (count, core_rows), 1)
    core = own_group()
    x, y = place_on(place // rows % SIDE, place // (rows * SIDE), core)
    wanted = device(y, x, core) * rows + place % rows
    picked = jnp.dot(
        digits.astype(F32).astype(BF16),
        (source == wanted).astype(F32).astype(BF16),
        preferred_element_type=F32,
    )
    targets = picked[0:1] + 256.0 * picked[1:2] + 65536.0 * picked[2:3]
    targets = by_distance(jnp.broadcast_to(targets, (STAT_ROWS, core_rows)), rows)
    targets_out_ref[...] = targets[:1].astype(jnp.int32)


def normed_kernel(features_ref, gain_ref, out_ref, inv_ref):
    parts, rows, width = features_ref.shape
    squares = sum(
        jnp.sum(features_ref[k] * features_ref[k], axis=1, keepdims=True) for k in range(parts)
    )
    inv_rms = lax.rsqrt(squares / (parts * width) + EPSILON)
    inv_ref[...] = jnp.broadcast_to(inv_rms, inv_ref.shape)
    for k in range(parts):
        columns = slice(k * width, (k + 1) * width)
        normed = features_ref[k] * inv_rms * gain_ref[:, columns]
        out_ref[:, columns] = normed.astype(out_ref.dtype)


def places_in(targets_ref, n_z, voc_dev, block):
    core = lax.axis_index("c")
    owner = core if block == 0 else 1 - core
    start = ((2 * plane_index() + owner) * n_z + lax.axis_index("z")) * voc_dev
    return targets_ref[...] - start


def is_target(places, shape):
    return lax.broadcasted_iota(jnp.int32, shape, 0) == places


def logits_kernel(
    n_z, rows_ref, own_ref, sib_ref, targets_ref, extra_ref,
    own_logits_ref, sib_logits_ref, out_ref, top_ref, own_stats_ref,
):
    for weight_ref, logits_ref in ((own_ref, own_logits_ref), (sib_ref, sib_logits_ref)):
        logits_ref[...] = lax.dot_general(
            weight_ref[...], rows_ref[...], CONTRACT_LAST, preferred_element_type=F32
        )
    parts = [own_logits_ref[...], sib_logits_ref[...]]
    top = jnp.maximum(*[jnp.max(part, axis=0, keepdims=True) for part in parts])
    total = sum(jnp.sum(jnp.exp(part - top), axis=0, keepdims=True) for part in parts)
    weighted = sum(jnp.sum(jnp.exp(part - top) * part, axis=0, keepdims=True) for part in parts)
    picked = jnp.zeros_like(top)
    for block, part in enumerate(parts):
        hot = is_target(places_in(targets_ref, n_z, part.shape[0], block), part.shape)
        picked += jnp.sum(jnp.where(hot, part, 0.0), axis=0, keepdims=True)
    top_ref[...] = jnp.broadcast_to(top, top_ref.shape)
    row = lax.broadcasted_iota(jnp.int32, top_ref.shape, 0)
    stats = jnp.where(row == 1, total, jnp.where(row == 2, picked, top))
    stats = jnp.where(row == 6, weighted, stats)
    stats = in_order(stats, rows_ref.shape[0] // (SIDE * SIDE))
    stats = jnp.where((row == 3) | (row == 4), extra_ref[...], stats)
    own_stats_ref[...] = stats
    for k in range(out_ref.shape[0]):
        out_ref[k] = stats


def sums_kernel(
    n_z, own_logits_ref, sib_logits_ref, top_ref, targets_ref, own_ref, sib_ref,
    ahead_ref, behind_ref, own_rest_ref, sib_rest_ref, *coefs,
):
    rows = own_logits_ref.shape[1]
    size = rows // SIDE
    rests = (own_rest_ref, sib_rest_ref)
    for block, (logits_ref, coef_ref) in enumerate(zip((own_logits_ref, sib_logits_ref), coefs)):
        logits = logits_ref[...]
        hot = is_target(places_in(targets_ref, n_z, logits.shape[0], block), logits.shape)
        powers = jnp.where(hot, 0.0, jnp.exp(logits - top_ref[0:1, :])).T
        hot = hot.astype(F32).T
        for k in range(SIDE):
            target_ref = (rests[block], coef_ref)[k % 2]
            start = k // 2 * 2 * size
            part = slice(k * size, (k + 1) * size)
            target_ref[start : start + size, :] = powers[part].astype(BF16)
            target_ref[start + size : start + 2 * size, :] = hot[part].astype(BF16)
    sums = products(coefs, (own_ref, sib_ref))
    ahead_ref[...] = sums[: 2 * size].astype(BF16)
    behind_ref[...] = sums[2 * size :].astype(BF16)


def products(coefs, weights):
    return sum(
        lax.dot_general(
            coef_ref[...], weight_ref[...], CONTRACT_MIDDLE, preferred_element_type=F32
        )
        for coef_ref, weight_ref in zip(coefs, weights)
    )


def rest_kernel(own_rest_ref, sib_rest_ref, own_ref, sib_ref, own_power_ref, own_hot_ref, far_ref):
    size = own_power_ref.shape[0]
    sums = products((own_rest_ref, sib_rest_ref), (own_ref, sib_ref))
    own_power_ref[...] = sums[:size]
    own_hot_ref[...] = sums[size : 2 * size].astype(BF16)
    far_ref[...] = sums[2 * size :].astype(BF16)


def merged(got_ref):
    senders = got_ref.shape[0]
    top = got_ref[0, 0:1, :]
    for k in range(1, senders):
        top = jnp.maximum(top, got_ref[k, 0:1, :])
    total, picked, weighted = [jnp.zeros_like(top)] * 3
    for k in range(senders):
        scale = jnp.exp(got_ref[k, 0:1, :] - top)
        total += got_ref[k, 1:2, :] * scale
        weighted += got_ref[k, 6:7, :] * scale
        picked += got_ref[k, 2:3, :]
    return top, total, picked, weighted


def merge_kernel(got_ref, own_ref, out_ref):
    top, total, picked, weighted = merged(got_ref)
    row = lax.broadcasted_iota(jnp.int32, own_ref.shape, 0)
    stats = own_ref[...]
    for i, value in ((0, top), (1, total), (2, picked), (6, weighted)):
        stats = jnp.where(row == i, value, stats)
    for k in range(out_ref.shape[0]):
        out_ref[k] = stats


def totals_kernel(got_ref, part_ref, dots_ref):
    rows, lanes = part_ref.shape
    top, total, picked, weighted = merged(got_ref)
    entries = got_ref[0]
    for k in range(1, got_ref.shape[0]):
        entries += got_ref[k]
    log_total = top + jnp.log(total)
    ratio = (picked - log_total - entries[3:4, :]) * entries[4:5, :]
    part_ref[...] = jnp.broadcast_to(jnp.sum(ratio, axis=1, keepdims=True), part_ref.shape)
    dots = jnp.broadcast_to(picked - weighted / total, (STAT_ROWS, lanes))
    dots_ref[...] = columns_of(by_distance(dots, rows)[0:1, :], rows)


def outer_kernel(got_ref, own_power_ref, own_hot_ref, *refs):
    blocks, (out_ref, scale_ref, total_ref) = refs[: SIDE - 1], refs[SIDE - 1 :]
    size = own_power_ref.shape[0]
    rows = size // SIDE
    parts = out_ref.shape[0] // SIDE
    width = out_ref.shape[2]
    outer, inner = own_place()
    core = own_group()
    top, total, picked, _ = merged(got_ref)
    log_total = top + jnp.log(total)
    shape = got_ref.shape[1:]
    hot_factor = by_distance(jnp.broadcast_to(1.0 - jnp.exp(picked - log_total), shape), rows)
    scale_ref[SIDE] = columns_of(hot_factor[0:1, :], size)
    for k in range(SIDE):
        x, y = place_on(inner, (outer + SIDE - k) % SIDE, core)
        scale = jnp.exp(got_ref[y * SIDE + x] - log_total)
        scale_ref[k] = columns_of(by_distance(scale, rows)[5:6, :], size)
    for z in range(parts):
        for j in range(width // LANES):
            columns = slice(z * width + j * LANES, z * width + (j + 1) * LANES)
            power = scale_ref[0] * own_power_ref[:, columns]
            hot = own_hot_ref[:, columns].astype(F32)
            for k in range(1, SIDE):
                power += scale_ref[k] * blocks[k - 1][:size, columns].astype(F32)
                hot += blocks[k - 1][size:, columns].astype(F32)
            total_ref[:, j * LANES : (j + 1) * LANES] = scale_ref[SIDE] * hot - power
        for m in range(SIDE):
            term = total_ref[m * rows : (m + 1) * rows, :]
            out_ref[(inner + m) % SIDE * parts + z] = term.astype(out_ref.dtype)


def final_kernel(
    full_width, last_ref, hidden_ref, gain_ref, inv_ref, live_ref, dots_ref, own_part_ref,
    sib_part_ref, loss_ref, out_ref,
):
    rows, width = out_ref.shape
    term = last_ref[0].astype(F32)
    for k in range(1, last_ref.shape[0]):
        term += last_ref[k].astype(F32)
    own = pl.ds(pl.multiple_of(lax.axis_index("z") * width, width), width)
    value = -DPO_BETA * (own_part_ref[...] + sib_part_ref[...])
    loss = jnp.maximum(value, 0.0) + jnp.log1p(jnp.exp(-jnp.abs(value)))
    loss_ref[...] = loss[:1, :1]
    slope = -DPO_BETA / (1.0 + jnp.exp(-value))
    row_grad = (slope * live_ref[...])[:, :1]
    inv_rms = inv_ref[:, :1]
    row_dot = row_grad * (dots_ref[:, :1] / inv_rms) / full_width
    input_grad = inv_rms * (row_grad * (term * gain_ref[:, own])) - hidden_ref[...] * (
        inv_rms * inv_rms * inv_rms * row_dot
    )
    out_ref[...] = (LOSS_SCALE * input_grad).astype(out_ref.dtype)


def along_plane(value):
    groups = [
        [device(y, x, group) for y in range(SIDE) for x in range(SIDE)] for group in range(2)
    ]
    return lax.all_to_all(value, CTX, 0, 0, axis_index_groups=groups, tiled=True)


def along_inner_and_z(value, n_z):
    groups = [
        [
            device(*((inner, outer) if core == 0 else (outer, inner)), core) * n_z + z
            for inner in range(SIDE)
            for z in range(n_z)
        ]
        for core in range(2)
        for outer in range(SIDE)
    ]
    return lax.all_to_all(
        value, CTX + ("z",), 0, 0, axis_index_groups=groups, tiled=True
    )


def on_device(hidden, norm_gain, head_weight, targets, ref_logprobs, block_order, lengths):
    tok_dev, part_width = hidden.shape
    voc_dev, full_width = head_weight.shape
    n_plane = lax.axis_size(PLANE)
    n_z = lax.axis_size("z")
    half = tok_dev * n_plane
    block = half // SIDE
    rows_in_all = targets.shape[0]
    flops = 4 * half * voc_dev * full_width
    moved = 4 * (voc_dev + half) * full_width

    sib_weight = other_core(head_weight)
    sent, hidden_f32, gain, targets, live_rows, extra = run(
        prepare_kernel,
        [
            ((n_z * tok_dev, part_width), BF16),
            ((tok_dev, part_width), F32),
            ((1, full_width), F32),
            ((1, half), jnp.int32),
            ((tok_dev, LANES), F32),
            ((STAT_ROWS, half), F32),
        ],
        [
            pltpu.VMEM((tok_dev, part_width), BF16),
            pltpu.VMEM((1, rows_in_all), jnp.int32),
            pltpu.SMEM((tok_dev,), F32),
            pltpu.SMEM((2,), jnp.int32),
            pltpu.SMEM((2,), jnp.int32),
            pltpu.SemaphoreType.DMA((6,)),
        ],
        *[
            pltpu.with_memory_space_constraint(value, pltpu.HBM)
            for value in (
                hidden, norm_gain[None, :], targets[None, :], ref_logprobs, block_order, lengths
            )
        ],
        specs=[IN_HBM] * 6,
        moved=1 << 20,
    )
    sent = sent.reshape(n_z, tok_dev, part_width)

    features = exchange(sent, "z").astype(F32)
    normed, inv_rms = run(
        normed_kernel,
        [((tok_dev, full_width), BF16), ((tok_dev, LANES), F32)],
        [],
        features,
        gain,
        moved=2 * half * full_width,
    )
    normed, sib_weight = lax.optimization_barrier((normed, sib_weight))
    own_weight = other_core(sib_weight)
    sib_weight = pltpu.with_memory_space_constraint(sib_weight, pltpu.VMEM)
    nearby = gather_from(normed, False)
    rows = gather_from(nearby, True)
    own_logits, sib_logits, stats, tops, own_stats = run(
        functools.partial(logits_kernel, n_z),
        [
            ((voc_dev, half), F32),
            ((voc_dev, half), F32),
            ((n_z, STAT_ROWS, half), F32),
            ((STAT_ROWS, half), F32),
            ((STAT_ROWS, half), F32),
        ],
        [],
        rows,
        own_weight,
        sib_weight,
        targets,
        extra,
        flops=flops,
        moved=moved,
    )
    ahead, behind, own_rest, sib_rest = run(
        functools.partial(sums_kernel, n_z),
        [((2 * block, full_width), BF16)] * 2 + [((half, voc_dev), BF16)] * 2,
        [pltpu.VMEM((half, voc_dev), BF16)] * 2,
        own_logits,
        sib_logits,
        tops,
        targets,
        own_weight,
        sib_weight,
        flops=flops,
        moved=moved,
    )
    ahead, behind = from_ahead(ahead, 3, True), from_ahead(behind, 1, True)
    own_power, own_hot, far = run(
        rest_kernel,
        [
            ((block, full_width), F32),
            ((block, full_width), BF16),
            ((2 * block, full_width), BF16),
        ],
        [],
        own_rest,
        sib_rest,
        own_weight,
        sib_weight,
        flops=flops,
        moved=moved,
    )
    stats, far = lax.optimization_barrier((stats, far))
    blocks = [ahead, from_ahead(far, 2, True), behind]
    (stats,) = run(
        merge_kernel,
        [((n_plane, STAT_ROWS, half), F32)],
        [],
        exchange(stats, "z"),
        own_stats,
        moved=1 << 17,
    )
    got = along_plane(stats)
    own_part, dots = run(
        totals_kernel, [((tok_dev, LANES), F32)] * 2, [], got, moved=1 << 17
    )
    sib_part = other_core(own_part)
    (last,) = run(
        outer_kernel,
        [((SIDE * n_z, tok_dev, part_width), BF16)],
        [pltpu.VMEM((SIDE + 1, block, half), F32), pltpu.VMEM((block, part_width), F32)],
        got,
        own_power,
        own_hot,
        *blocks,
        moved=8 * half * full_width,
    )
    last, sib_part = lax.optimization_barrier((last, sib_part))
    last = along_inner_and_z(last, n_z)
    loss, hidden_grad = pl.pallas_call(
        functools.partial(final_kernel, full_width),
        in_specs=[IN_VMEM] * 8,
        out_specs=[IN_VMEM] * 2,
        out_shape=[
            jax.ShapeDtypeStruct((1, 1), F32),
            jax.ShapeDtypeStruct((tok_dev, part_width), BF16),
        ],
        compiler_params=pltpu.CompilerParams(vmem_limit_bytes=VMEM_LIMIT),
    )(last, hidden_f32, gain, inv_rms, live_rows, dots, own_part, sib_part)
    return (loss[0, 0], hidden_grad)


def solution(mesh):
    fine = Mesh(mesh.devices.reshape(SIDE, SIDE, 2, 8), ("y", "x", "c", "z"))
    placed = (P(CTX, "z"), P(), P(CTX + ("z",), None), P(), P(CTX), P(CTX), P())
    return jax.shard_map(
        on_device, mesh=fine, in_specs=placed, out_specs=(P(), P(CTX, "z")), check_vma=False
    )
```

```python
import functools

import jax
import jax.numpy as jnp
from jax import lax
from jax.experimental import pallas as pl
from jax.experimental.pallas import tpu as pltpu
from jax.sharding import Mesh, PartitionSpec as P

EPSILON = 1e-05
DPO_BETA = 0.05
LOSS_SCALE = 4096.0
PLANE = ("y", "x")
CTX = ("y", "x", "c")
CHUNK = 2048
LANES = 128
STAT_ROWS = 8
SIDE = 4
VMEM_LIMIT = 16 * 1024 * 1024
CONTRACT_LAST = (((1,), (1,)), ((), ()))
CONTRACT_MIDDLE = (((1,), (0,)), ((), ()))
F32, BF16 = jnp.float32, jnp.bfloat16


def other_core(value):
    return lax.ppermute(value, "c", [(0, 1), (1, 0)])


def exchange(value, axes):
    return lax.all_to_all(value, axes, 0, 0, tiled=True)


IN_VMEM = pl.BlockSpec(memory_space=pltpu.VMEM)
IN_SMEM = pl.BlockSpec(memory_space=pltpu.SMEM)
IN_HBM = pl.BlockSpec(memory_space=pltpu.HBM)


def run(kernel, outputs, scratch, *operands, specs=None, flops=0, moved=0):
    return pl.pallas_call(
        kernel,
        in_specs=specs or [IN_VMEM] * len(operands),
        out_specs=[IN_VMEM] * len(outputs),
        out_shape=[pltpu.VMEM(shape, dtype) for shape, dtype in outputs],
        scratch_shapes=scratch,
        compiler_params=pltpu.CompilerParams(vmem_limit_bytes=VMEM_LIMIT),
        cost_estimate=pl.CostEstimate(flops=flops, bytes_accessed=moved, transcendentals=0),
    )(*operands)


def plane_index():
    return lax.axis_index("y") * lax.axis_size("x") + lax.axis_index("x")


def own_group():
    return (lax.axis_index("c") + lax.axis_index("x") + lax.axis_index("y")) % 2


def place_on(y, x, group):
    return (jnp.where(group == 0, x, y), jnp.where(group == 0, y, x))


def own_place():
    return place_on(lax.axis_index("y"), lax.axis_index("x"), own_group())


def device(y, x, group):
    return (y * SIDE + x) * 2 + (group + x + y) % 2


def from_ahead(value, step, outer):
    pairs = []
    for y in range(SIDE):
        for x in range(SIDE):
            for core in range(2):
                if (core == 0) == outer:
                    source = device(y, (x + step) % SIDE, core)
                else:
                    source = device((y + step) % SIDE, x, core)
                pairs.append((source, device(y, x, core)))
    return lax.ppermute(value, CTX, pairs)


def gather_from(value, outer):
    far = from_ahead(value, 2, outer)
    return jnp.concatenate(
        [value, from_ahead(value, 1, outer), far, from_ahead(value, 3, outer)], axis=0
    )


def by_distance(value, rows):
    lanes = value.shape[1]
    group = SIDE * rows
    outer, inner = own_place()
    value = pltpu.roll(value, (lanes - outer * group) % lanes, 1)
    lane = lax.broadcasted_iota(jnp.int32, value.shape, 1)
    shift = inner * rows
    behind = pltpu.roll(value, (lanes - shift) % lanes, 1)
    wrapped = pltpu.roll(value, (lanes - shift + group) % lanes, 1)
    return jnp.where(lane % group < group - shift, behind, wrapped)


def columns_of(row, rows):
    lanes = row.shape[1]
    return jnp.broadcast_to(row, (lanes, lanes)).T[:rows]


def in_order(value, rows):
    lanes = value.shape[1]
    group = SIDE * rows
    outer, inner = own_place()
    lane = lax.broadcasted_iota(jnp.int32, value.shape, 1)
    shift = inner * rows
    ahead = pltpu.roll(value, shift, 1)
    wrapped = pltpu.roll(value, (shift + lanes - group) % lanes, 1)
    value = jnp.where(lane % group >= shift, ahead, wrapped)
    return pltpu.roll(value, outer * group, 1)


def prepare_kernel(
    hidden_hbm, gain_hbm, targets_hbm, logprobs_hbm, order_hbm, lengths_hbm,
    sent_ref, hidden_out_ref, gain_out_ref, targets_out_ref, live_ref, extra_ref,
    hidden_ref, targets_ref, logprobs_ref, order_ref, lengths_ref, sems,
):
    copies = [
        pltpu.make_async_copy(source, target, sems.at[i])
        for i, (source, target) in enumerate(
            (
                (hidden_hbm, hidden_ref),
                (gain_hbm, gain_out_ref),
                (targets_hbm, targets_ref),
                (logprobs_hbm, logprobs_ref),
                (order_hbm, order_ref),
                (lengths_hbm, lengths_ref),
            )
        )
    ]
    for copy in copies:
        copy.start()
    for copy in copies:
        copy.wait()
    rows = hidden_ref.shape[0]
    core_rows = extra_ref.shape[1]
    hidden = hidden_ref[...].astype(F32)
    hidden_out_ref[...] = hidden
    twice = jnp.concatenate([hidden, hidden], axis=0).astype(sent_ref.dtype)
    for i in range(sent_ref.shape[0] // (2 * rows)):
        sent_ref[i * 2 * rows : (i + 1) * 2 * rows, :] = twice

    def live_sign(row):
        block_len = rows // 4
        rejected = row // (2 * block_len) == 1
        second = row // block_len % 2 == 1
        start = jnp.where(second, order_ref[1], order_ref[0])
        limit = jnp.where(rejected, lengths_ref[1], lengths_ref[0])
        live = start * block_len + row % block_len < limit
        return jnp.where(live, jnp.where(rejected, -1.0, 1.0), 0.0)

    live_ref[...] = live_sign(lax.broadcasted_iota(jnp.int32, live_ref.shape, 0))
    lane = lax.broadcasted_iota(jnp.int32, (1, core_rows), 1)
    outer, inner = own_place()
    mine = lane // rows == outer * SIDE + inner
    logprobs = jnp.zeros((1, core_rows), F32)
    for t in range(rows):
        logprobs = jnp.where(lane % rows == t, logprobs_ref[t], logprobs)
    extra_ref[...] = jnp.zeros_like(extra_ref)
    extra_ref[3:4, :] = jnp.where(mine, logprobs, 0.0)
    extra_ref[4:5, :] = jnp.where(mine, live_sign(lane % rows), 0.0)
    count = targets_ref.shape[1]
    digit = jnp.minimum(lax.broadcasted_iota(jnp.int32, (STAT_ROWS, count), 0), 3)
    digits = lax.shift_right_logical(
        jnp.broadcast_to(targets_ref[...], (STAT_ROWS, count)), 8 * digit
    ) & 255
    source = lax.broadcasted_iota(jnp.int32, (count, core_rows), 0)
    place = lax.broadcasted_iota(jnp.int32, (count, core_rows), 1)
    core = own_group()
    x, y = place_on(place // rows % SIDE, place // (rows * SIDE), core)
    wanted = device(y, x, core) * rows + place % rows
    picked = jnp.dot(
        digits.astype(F32).astype(BF16),
        (source == wanted).astype(F32).astype(BF16),
        preferred_element_type=F32,
    )
    targets = picked[0:1] + 256.0 * picked[1:2] + 65536.0 * picked[2:3]
    targets = by_distance(jnp.broadcast_to(targets, (STAT_ROWS, core_rows)), rows)
    targets_out_ref[...] = targets[:1].astype(jnp.int32)


def normed_kernel(features_ref, gain_ref, out_ref, inv_ref):
    parts, rows, width = features_ref.shape
    squares = sum(
        jnp.sum(features_ref[k] * features_ref[k], axis=1, keepdims=True) for k in range(parts)
    )
    inv_rms = lax.rsqrt(squares / (parts * width) + EPSILON)
    inv_ref[...] = jnp.broadcast_to(inv_rms, inv_ref.shape)
    for k in range(parts):
        columns = slice(k * width, (k + 1) * width)
        normed = features_ref[k] * inv_rms * gain_ref[:, columns]
        out_ref[:, columns] = normed.astype(out_ref.dtype)


def places_in(targets_ref, n_z, voc_dev, block):
    core = lax.axis_index("c")
    owner = core if block == 0 else 1 - core
    start = ((2 * plane_index() + owner) * n_z + lax.axis_index("z")) * voc_dev
    return targets_ref[...] - start


def is_target(places, shape):
    return lax.broadcasted_iota(jnp.int32, shape, 0) == places


def logits_kernel(
    n_z, rows_ref, own_ref, sib_ref, targets_ref, extra_ref,
    own_logits_ref, sib_logits_ref, out_ref, top_ref, own_stats_ref,
):
    for weight_ref, logits_ref in ((own_ref, own_logits_ref), (sib_ref, sib_logits_ref)):
        logits_ref[...] = lax.dot_general(
            weight_ref[...], rows_ref[...], CONTRACT_LAST, preferred_element_type=F32
        )
    parts = [own_logits_ref[...], sib_logits_ref[...]]
    top = jnp.maximum(*[jnp.max(part, axis=0, keepdims=True) for part in parts])
    total = sum(jnp.sum(jnp.exp(part - top), axis=0, keepdims=True) for part in parts)
    weighted = sum(jnp.sum(jnp.exp(part - top) * part, axis=0, keepdims=True) for part in parts)
    picked = jnp.zeros_like(top)
    for block, part in enumerate(parts):
        hot = is_target(places_in(targets_ref, n_z, part.shape[0], block), part.shape)
        picked += jnp.sum(jnp.where(hot, part, 0.0), axis=0, keepdims=True)
    top_ref[...] = jnp.broadcast_to(top, top_ref.shape)
    row = lax.broadcasted_iota(jnp.int32, top_ref.shape, 0)
    stats = jnp.where(row == 1, total, jnp.where(row == 2, picked, top))
    stats = jnp.where(row == 6, weighted, stats)
    stats = in_order(stats, rows_ref.shape[0] // (SIDE * SIDE))
    stats = jnp.where((row == 3) | (row == 4), extra_ref[...], stats)
    own_stats_ref[...] = stats
    for k in range(out_ref.shape[0]):
        out_ref[k] = stats


def sums_kernel(
    n_z, own_logits_ref, sib_logits_ref, top_ref, targets_ref, own_ref, sib_ref,
    ahead_ref, behind_ref, own_rest_ref, sib_rest_ref, *coefs,
):
    rows = own_logits_ref.shape[1]
    size = rows // SIDE
    rests = (own_rest_ref, sib_rest_ref)
    for block, (logits_ref, coef_ref) in enumerate(zip((own_logits_ref, sib_logits_ref), coefs)):
        logits = logits_ref[...]
        hot = is_target(places_in(targets_ref, n_z, logits.shape[0], block), logits.shape)
        powers = jnp.where(hot, 0.0, jnp.exp(logits - top_ref[0:1, :])).T
        hot = hot.astype(F32).T
        for k in range(SIDE):
            target_ref = (rests[block], coef_ref)[k % 2]
            start = k // 2 * 2 * size
            part = slice(k * size, (k + 1) * size)
            target_ref[start : start + size, :] = powers[part].astype(BF16)
            target_ref[start + size : start + 2 * size, :] = hot[part].astype(BF16)
    sums = products(coefs, (own_ref, sib_ref))
    ahead_ref[...] = sums[: 2 * size].astype(BF16)
    behind_ref[...] = sums[2 * size :].astype(BF16)


def products(coefs, weights):
    return sum(
        lax.dot_general(
            coef_ref[...], weight_ref[...], CONTRACT_MIDDLE, preferred_element_type=F32
        )
        for coef_ref, weight_ref in zip(coefs, weights)
    )


def rest_kernel(
    own_rest_ref, sib_rest_ref, own_ref, sib_ref, own_power_ref, own_hot_ref, far_power_ref, far_hot_ref
):
    size = own_power_ref.shape[0]
    sums = products((own_rest_ref, sib_rest_ref), (own_ref, sib_ref))
    own_power_ref[...] = sums[:size]
    own_hot_ref[...] = sums[size : 2 * size].astype(BF16)
    far_power_ref[...] = sums[2 * size : 3 * size].astype(BF16)
    far_hot_ref[...] = sums[3 * size :].astype(BF16)


def merged(got_ref):
    senders = got_ref.shape[0]
    top = got_ref[0, 0:1, :]
    for k in range(1, senders):
        top = jnp.maximum(top, got_ref[k, 0:1, :])
    total, picked, weighted = [jnp.zeros_like(top)] * 3
    for k in range(senders):
        scale = jnp.exp(got_ref[k, 0:1, :] - top)
        total += got_ref[k, 1:2, :] * scale
        weighted += got_ref[k, 6:7, :] * scale
        picked += got_ref[k, 2:3, :]
    return top, total, picked, weighted


def merge_kernel(got_ref, own_ref, out_ref):
    top, total, picked, weighted = merged(got_ref)
    row = lax.broadcasted_iota(jnp.int32, own_ref.shape, 0)
    stats = own_ref[...]
    for i, value in ((0, top), (1, total), (2, picked), (6, weighted)):
        stats = jnp.where(row == i, value, stats)
    for k in range(out_ref.shape[0]):
        out_ref[k] = stats


def totals_kernel(got_ref, part_ref, dots_ref):
    rows, lanes = part_ref.shape
    top, total, picked, weighted = merged(got_ref)
    entries = got_ref[0]
    for k in range(1, got_ref.shape[0]):
        entries += got_ref[k]
    log_total = top + jnp.log(total)
    ratio = (picked - log_total - entries[3:4, :]) * entries[4:5, :]
    part_ref[...] = jnp.broadcast_to(jnp.sum(ratio, axis=1, keepdims=True), part_ref.shape)
    dots = jnp.broadcast_to(picked - weighted / total, (STAT_ROWS, lanes))
    dots_ref[...] = columns_of(by_distance(dots, rows)[0:1, :], rows)


def outer_kernel(
    got_ref, own_power_ref, own_hot_ref, ahead_ref, far_power_ref, far_hot_ref, behind_ref,
    out_ref, scale_ref, total_ref,
):
    size = own_power_ref.shape[0]
    rows = size // SIDE
    parts = out_ref.shape[0] // SIDE
    width = out_ref.shape[2]
    outer, inner = own_place()
    core = own_group()
    top, total, picked, _ = merged(got_ref)
    log_total = top + jnp.log(total)
    shape = got_ref.shape[1:]
    hot_factor = by_distance(jnp.broadcast_to(1.0 - jnp.exp(picked - log_total), shape), rows)
    scale_ref[SIDE] = columns_of(hot_factor[0:1, :], size)
    for k in range(SIDE):
        x, y = place_on(inner, (outer + SIDE - k) % SIDE, core)
        scale = jnp.exp(got_ref[y * SIDE + x] - log_total)
        scale_ref[k] = columns_of(by_distance(scale, rows)[5:6, :], size)
    for z in range(parts):
        for j in range(width // LANES):
            columns = slice(z * width + j * LANES, z * width + (j + 1) * LANES)
            power = scale_ref[0] * own_power_ref[:, columns]
            hot = own_hot_ref[:, columns].astype(F32)
            for k, block_ref in ((1, ahead_ref), (3, behind_ref)):
                power += scale_ref[k] * block_ref[:size, columns].astype(F32)
                hot += block_ref[size:, columns].astype(F32)
            power += scale_ref[2] * far_power_ref[:, columns].astype(F32)
            hot += far_hot_ref[:, columns].astype(F32)
            total_ref[:, j * LANES : (j + 1) * LANES] = scale_ref[SIDE] * hot - power
        for m in range(SIDE):
            term = total_ref[m * rows : (m + 1) * rows, :]
            out_ref[(inner + m) % SIDE * parts + z] = term.astype(out_ref.dtype)


def final_kernel(
    full_width, last_ref, hidden_ref, gain_ref, inv_ref, live_ref, dots_ref, own_part_ref,
    sib_part_ref, loss_ref, out_ref,
):
    rows, width = out_ref.shape
    term = last_ref[0].astype(F32)
    for k in range(1, last_ref.shape[0]):
        term += last_ref[k].astype(F32)
    own = pl.ds(pl.multiple_of(lax.axis_index("z") * width, width), width)
    value = -DPO_BETA * (own_part_ref[...] + sib_part_ref[...])
    loss = jnp.maximum(value, 0.0) + jnp.log1p(jnp.exp(-jnp.abs(value)))
    loss_ref[...] = loss[:1, :1]
    slope = -DPO_BETA / (1.0 + jnp.exp(-value))
    row_grad = (slope * live_ref[...])[:, :1]
    inv_rms = inv_ref[:, :1]
    row_dot = row_grad * (dots_ref[:, :1] / inv_rms) / full_width
    input_grad = inv_rms * (row_grad * (term * gain_ref[:, own])) - hidden_ref[...] * (
        inv_rms * inv_rms * inv_rms * row_dot
    )
    out_ref[...] = (LOSS_SCALE * input_grad).astype(out_ref.dtype)


def along_plane(value):
    groups = [
        [device(y, x, group) for y in range(SIDE) for x in range(SIDE)] for group in range(2)
    ]
    return lax.all_to_all(value, CTX, 0, 0, axis_index_groups=groups, tiled=True)


def along_inner_and_z(value, n_z):
    groups = [
        [
            device(*((inner, outer) if core == 0 else (outer, inner)), core) * n_z + z
            for inner in range(SIDE)
            for z in range(n_z)
        ]
        for core in range(2)
        for outer in range(SIDE)
    ]
    return lax.all_to_all(
        value, CTX + ("z",), 0, 0, axis_index_groups=groups, tiled=True
    )


def on_device(hidden, norm_gain, head_weight, targets, ref_logprobs, block_order, lengths):
    tok_dev, part_width = hidden.shape
    voc_dev, full_width = head_weight.shape
    n_plane = lax.axis_size(PLANE)
    n_z = lax.axis_size("z")
    half = tok_dev * n_plane
    block = half // SIDE
    rows_in_all = targets.shape[0]
    flops = 4 * half * voc_dev * full_width
    moved = 4 * (voc_dev + half) * full_width

    sib_weight = other_core(head_weight)
    sent, hidden_f32, gain, targets, live_rows, extra = run(
        prepare_kernel,
        [
            ((n_z * tok_dev, part_width), BF16),
            ((tok_dev, part_width), F32),
            ((1, full_width), F32),
            ((1, half), jnp.int32),
            ((tok_dev, LANES), F32),
            ((STAT_ROWS, half), F32),
        ],
        [
            pltpu.VMEM((tok_dev, part_width), BF16),
            pltpu.VMEM((1, rows_in_all), jnp.int32),
            pltpu.SMEM((tok_dev,), F32),
            pltpu.SMEM((2,), jnp.int32),
            pltpu.SMEM((2,), jnp.int32),
            pltpu.SemaphoreType.DMA((6,)),
        ],
        *[
            pltpu.with_memory_space_constraint(value, pltpu.HBM)
            for value in (
                hidden, norm_gain[None, :], targets[None, :], ref_logprobs, block_order, lengths
            )
        ],
        specs=[IN_HBM] * 6,
        moved=1 << 20,
    )
    sent = sent.reshape(n_z, tok_dev, part_width)

    features = exchange(sent, "z").astype(F32)
    normed, inv_rms = run(
        normed_kernel,
        [((tok_dev, full_width), BF16), ((tok_dev, LANES), F32)],
        [],
        features,
        gain,
        moved=2 * half * full_width,
    )
    normed, sib_weight = lax.optimization_barrier((normed, sib_weight))
    own_weight = other_core(sib_weight)
    sib_weight = pltpu.with_memory_space_constraint(sib_weight, pltpu.VMEM)
    nearby = gather_from(normed, False)
    rows = jnp.concatenate(
        [
            nearby,
            from_ahead(nearby, 1, True),
            from_ahead(nearby[: block // 2], 2, True),
            from_ahead(nearby[block // 2 :], 2, True),
            from_ahead(nearby, 3, True),
        ],
        axis=0,
    )
    own_logits, sib_logits, stats, tops, own_stats = run(
        functools.partial(logits_kernel, n_z),
        [
            ((voc_dev, half), F32),
            ((voc_dev, half), F32),
            ((n_z, STAT_ROWS, half), F32),
            ((STAT_ROWS, half), F32),
            ((STAT_ROWS, half), F32),
        ],
        [],
        rows,
        own_weight,
        sib_weight,
        targets,
        extra,
        flops=flops,
        moved=moved,
    )
    ahead, behind, own_rest, sib_rest = run(
        functools.partial(sums_kernel, n_z),
        [((2 * block, full_width), BF16)] * 2 + [((half, voc_dev), BF16)] * 2,
        [pltpu.VMEM((half, voc_dev), BF16)] * 2,
        own_logits,
        sib_logits,
        tops,
        targets,
        own_weight,
        sib_weight,
        flops=flops,
        moved=moved,
    )
    ahead, behind = from_ahead(ahead, 3, True), from_ahead(behind, 1, True)
    own_power, own_hot, far_power, far_hot = run(
        rest_kernel,
        [((block, full_width), F32)] + [((block, full_width), BF16)] * 3,
        [],
        own_rest,
        sib_rest,
        own_weight,
        sib_weight,
        flops=flops,
        moved=moved,
    )
    stats, far_power, far_hot = lax.optimization_barrier((stats, far_power, far_hot))
    far_power, far_hot = [from_ahead(far, 2, True) for far in (far_power, far_hot)]
    (stats,) = run(
        merge_kernel,
        [((n_plane, STAT_ROWS, half), F32)],
        [],
        exchange(stats, "z"),
        own_stats,
        moved=1 << 17,
    )
    got = along_plane(stats)
    own_part, dots = run(
        totals_kernel, [((tok_dev, LANES), F32)] * 2, [], got, moved=1 << 17
    )
    sib_part = other_core(own_part)
    (last,) = run(
        outer_kernel,
        [((SIDE * n_z, tok_dev, part_width), BF16)],
        [pltpu.VMEM((SIDE + 1, block, half), F32), pltpu.VMEM((block, part_width), F32)],
        got,
        own_power,
        own_hot,
        ahead,
        far_power,
        far_hot,
        behind,
        moved=8 * half * full_width,
    )
    last, sib_part = lax.optimization_barrier((last, sib_part))
    last = along_inner_and_z(last, n_z)
    loss, hidden_grad = pl.pallas_call(
        functools.partial(final_kernel, full_width),
        in_specs=[IN_VMEM] * 8,
        out_specs=[IN_VMEM] * 2,
        out_shape=[
            jax.ShapeDtypeStruct((1, 1), F32),
            jax.ShapeDtypeStruct((tok_dev, part_width), BF16),
        ],
        compiler_params=pltpu.CompilerParams(vmem_limit_bytes=VMEM_LIMIT),
    )(last, hidden_f32, gain, inv_rms, live_rows, dots, own_part, sib_part)
    return (loss[0, 0], hidden_grad)


def solution(mesh):
    fine = Mesh(mesh.devices.reshape(SIDE, SIDE, 2, 8), ("y", "x", "c", "z"))
    placed = (P(CTX, "z"), P(), P(CTX + ("z",), None), P(), P(CTX), P(CTX), P())
    return jax.shard_map(
        on_device, mesh=fine, in_specs=placed, out_specs=(P(), P(CTX, "z")), check_vma=False
    )
```

```python
import functools

import jax
import jax.numpy as jnp
from jax import lax
from jax.experimental import pallas as pl
from jax.experimental.pallas import tpu as pltpu
from jax.sharding import Mesh, PartitionSpec as P

EPSILON = 1e-05
DPO_BETA = 0.05
LOSS_SCALE = 4096.0
PLANE = ("y", "x")
CTX = ("y", "x", "c")
CHUNK = 2048
LANES = 128
STAT_ROWS = 8
SIDE = 4
VMEM_LIMIT = 16 * 1024 * 1024
CONTRACT_LAST = (((1,), (1,)), ((), ()))
CONTRACT_MIDDLE = (((1,), (0,)), ((), ()))
F32, BF16 = jnp.float32, jnp.bfloat16


def other_core(value):
    return lax.ppermute(value, "c", [(0, 1), (1, 0)])


def exchange(value, axes):
    return lax.all_to_all(value, axes, 0, 0, tiled=True)


IN_VMEM = pl.BlockSpec(memory_space=pltpu.VMEM)
IN_SMEM = pl.BlockSpec(memory_space=pltpu.SMEM)
IN_HBM = pl.BlockSpec(memory_space=pltpu.HBM)


def run(kernel, outputs, scratch, *operands, specs=None, flops=0, moved=0):
    return pl.pallas_call(
        kernel,
        in_specs=specs or [IN_VMEM] * len(operands),
        out_specs=[IN_VMEM] * len(outputs),
        out_shape=[pltpu.VMEM(shape, dtype) for shape, dtype in outputs],
        scratch_shapes=scratch,
        compiler_params=pltpu.CompilerParams(vmem_limit_bytes=VMEM_LIMIT),
        cost_estimate=pl.CostEstimate(flops=flops, bytes_accessed=moved, transcendentals=0),
    )(*operands)


def plane_index():
    return lax.axis_index("y") * lax.axis_size("x") + lax.axis_index("x")


def own_group():
    return (lax.axis_index("c") + lax.axis_index("x") + lax.axis_index("y")) % 2


def place_on(y, x, group):
    return (jnp.where(group == 0, x, y), jnp.where(group == 0, y, x))


def own_place():
    return place_on(lax.axis_index("y"), lax.axis_index("x"), own_group())


def device(y, x, group):
    return (y * SIDE + x) * 2 + (group + x + y) % 2


def from_ahead(value, step, outer):
    pairs = []
    for y in range(SIDE):
        for x in range(SIDE):
            for core in range(2):
                if (core == 0) == outer:
                    source = device(y, (x + step) % SIDE, core)
                else:
                    source = device((y + step) % SIDE, x, core)
                pairs.append((source, device(y, x, core)))
    return lax.ppermute(value, CTX, pairs)


def gather_from(value, outer):
    far = from_ahead(value, 2, outer)
    return jnp.concatenate(
        [value, from_ahead(value, 1, outer), far, from_ahead(value, 3, outer)], axis=0
    )


def by_distance(value, rows):
    lanes = value.shape[1]
    group = SIDE * rows
    outer, inner = own_place()
    value = pltpu.roll(value, (lanes - outer * group) % lanes, 1)
    lane = lax.broadcasted_iota(jnp.int32, value.shape, 1)
    shift = inner * rows
    behind = pltpu.roll(value, (lanes - shift) % lanes, 1)
    wrapped = pltpu.roll(value, (lanes - shift + group) % lanes, 1)
    return jnp.where(lane % group < group - shift, behind, wrapped)


def columns_of(row, rows):
    lanes = row.shape[1]
    return jnp.broadcast_to(row, (lanes, lanes)).T[:rows]


def in_order(value, rows):
    lanes = value.shape[1]
    group = SIDE * rows
    outer, inner = own_place()
    lane = lax.broadcasted_iota(jnp.int32, value.shape, 1)
    shift = inner * rows
    ahead = pltpu.roll(value, shift, 1)
    wrapped = pltpu.roll(value, (shift + lanes - group) % lanes, 1)
    value = jnp.where(lane % group >= shift, ahead, wrapped)
    return pltpu.roll(value, outer * group, 1)


def prepare_kernel(
    hidden_hbm, gain_hbm, targets_hbm, logprobs_hbm, order_hbm, lengths_hbm,
    sent_ref, hidden_out_ref, gain_out_ref, targets_out_ref, live_ref, extra_ref,
    hidden_ref, targets_ref, logprobs_ref, order_ref, lengths_ref, sems,
):
    copies = [
        pltpu.make_async_copy(source, target, sems.at[i])
        for i, (source, target) in enumerate(
            (
                (hidden_hbm, hidden_ref),
                (gain_hbm, gain_out_ref),
                (targets_hbm, targets_ref),
                (logprobs_hbm, logprobs_ref),
                (order_hbm, order_ref),
                (lengths_hbm, lengths_ref),
            )
        )
    ]
    for copy in copies:
        copy.start()
    for copy in copies:
        copy.wait()
    rows = hidden_ref.shape[0]
    core_rows = extra_ref.shape[1]
    hidden = hidden_ref[...].astype(F32)
    hidden_out_ref[...] = hidden
    twice = jnp.concatenate([hidden, hidden], axis=0).astype(sent_ref.dtype)
    for i in range(sent_ref.shape[0] // (2 * rows)):
        sent_ref[i * 2 * rows : (i + 1) * 2 * rows, :] = twice

    def live_sign(row):
        block_len = rows // 4
        rejected = row // (2 * block_len) == 1
        second = row // block_len % 2 == 1
        start = jnp.where(second, order_ref[1], order_ref[0])
        limit = jnp.where(rejected, lengths_ref[1], lengths_ref[0])
        live = start * block_len + row % block_len < limit
        return jnp.where(live, jnp.where(rejected, -1.0, 1.0), 0.0)

    live_ref[...] = live_sign(lax.broadcasted_iota(jnp.int32, live_ref.shape, 0))
    lane = lax.broadcasted_iota(jnp.int32, (1, core_rows), 1)
    outer, inner = own_place()
    mine = lane // rows == outer * SIDE + inner
    logprobs = jnp.zeros((1, core_rows), F32)
    for t in range(rows):
        logprobs = jnp.where(lane % rows == t, logprobs_ref[t], logprobs)
    extra_ref[...] = jnp.zeros_like(extra_ref)
    extra_ref[3:4, :] = jnp.where(mine, logprobs, 0.0)
    extra_ref[4:5, :] = jnp.where(mine, live_sign(lane % rows), 0.0)
    count = targets_ref.shape[1]
    digit = jnp.minimum(lax.broadcasted_iota(jnp.int32, (STAT_ROWS, count), 0), 3)
    digits = lax.shift_right_logical(
        jnp.broadcast_to(targets_ref[...], (STAT_ROWS, count)), 8 * digit
    ) & 255
    source = lax.broadcasted_iota(jnp.int32, (count, core_rows), 0)
    place = lax.broadcasted_iota(jnp.int32, (count, core_rows), 1)
    core = own_group()
    x, y = place_on(place // rows % SIDE, place // (rows * SIDE), core)
    wanted = device(y, x, core) * rows + place % rows
    picked = jnp.dot(
        digits.astype(F32).astype(BF16),
        (source == wanted).astype(F32).astype(BF16),
        preferred_element_type=F32,
    )
    targets = picked[0:1] + 256.0 * picked[1:2] + 65536.0 * picked[2:3]
    targets = by_distance(jnp.broadcast_to(targets, (STAT_ROWS, core_rows)), rows)
    targets_out_ref[...] = targets[:1].astype(jnp.int32)


def normed_kernel(features_ref, gain_ref, out_ref, inv_ref):
    parts, rows, width = features_ref.shape
    squares = sum(
        jnp.sum(features_ref[k] * features_ref[k], axis=1, keepdims=True) for k in range(parts)
    )
    inv_rms = lax.rsqrt(squares / (parts * width) + EPSILON)
    inv_ref[...] = jnp.broadcast_to(inv_rms, inv_ref.shape)
    for k in range(parts):
        columns = slice(k * width, (k + 1) * width)
        normed = features_ref[k] * inv_rms * gain_ref[:, columns]
        out_ref[:, columns] = normed.astype(out_ref.dtype)


def load_kernel(weight_hbm, out_ref, sems):
    copies = []
    for k in range(sems.shape[0]):
        columns = pl.ds(k * CHUNK, CHUNK)
        copies.append(
            pltpu.make_async_copy(weight_hbm.at[:, columns], out_ref.at[:, columns], sems.at[k])
        )
    for copy in copies:
        copy.start()
    for copy in copies:
        copy.wait()


def places_in(targets_ref, n_z, voc_dev, block):
    core = lax.axis_index("c")
    owner = core if block == 0 else 1 - core
    start = ((2 * plane_index() + owner) * n_z + lax.axis_index("z")) * voc_dev
    return targets_ref[...] - start


def is_target(places, shape):
    return lax.broadcasted_iota(jnp.int32, shape, 0) == places


def logits_kernel(
    n_z, rows_ref, own_ref, sib_ref, targets_ref, extra_ref,
    own_logits_ref, sib_logits_ref, out_ref, top_ref, own_stats_ref,
):
    for weight_ref, logits_ref in ((own_ref, own_logits_ref), (sib_ref, sib_logits_ref)):
        logits_ref[...] = lax.dot_general(
            weight_ref[...], rows_ref[...], CONTRACT_LAST, preferred_element_type=F32
        )
    parts = [own_logits_ref[...], sib_logits_ref[...]]
    top = jnp.maximum(*[jnp.max(part, axis=0, keepdims=True) for part in parts])
    total = sum(jnp.sum(jnp.exp(part - top), axis=0, keepdims=True) for part in parts)
    weighted = sum(jnp.sum(jnp.exp(part - top) * part, axis=0, keepdims=True) for part in parts)
    picked = jnp.zeros_like(top)
    for block, part in enumerate(parts):
        hot = is_target(places_in(targets_ref, n_z, part.shape[0], block), part.shape)
        picked += jnp.sum(jnp.where(hot, part, 0.0), axis=0, keepdims=True)
    top_ref[...] = jnp.broadcast_to(top, top_ref.shape)
    row = lax.broadcasted_iota(jnp.int32, top_ref.shape, 0)
    stats = jnp.where(row == 1, total, jnp.where(row == 2, picked, top))
    stats = jnp.where(row == 6, weighted, stats)
    stats = in_order(stats, rows_ref.shape[0] // (SIDE * SIDE))
    stats = jnp.where((row == 3) | (row == 4), extra_ref[...], stats)
    own_stats_ref[...] = stats
    for k in range(out_ref.shape[0]):
        out_ref[k] = stats


def sums_kernel(
    n_z, own_logits_ref, sib_logits_ref, top_ref, targets_ref, own_ref, sib_ref,
    ahead_ref, behind_ref, own_rest_ref, sib_rest_ref, *coefs,
):
    rows = own_logits_ref.shape[1]
    size = rows // SIDE
    rests = (own_rest_ref, sib_rest_ref)
    for block, (logits_ref, coef_ref) in enumerate(zip((own_logits_ref, sib_logits_ref), coefs)):
        logits = logits_ref[...]
        hot = is_target(places_in(targets_ref, n_z, logits.shape[0], block), logits.shape)
        powers = jnp.where(hot, 0.0, jnp.exp(logits - top_ref[0:1, :])).T
        hot = hot.astype(F32).T
        for k in range(SIDE):
            target_ref = (rests[block], coef_ref)[k % 2]
            start = k // 2 * 2 * size
            part = slice(k * size, (k + 1) * size)
            target_ref[start : start + size, :] = powers[part].astype(BF16)
            target_ref[start + size : start + 2 * size, :] = hot[part].astype(BF16)
    sums = products(coefs, (own_ref, sib_ref))
    ahead_ref[...] = sums[: 2 * size].astype(BF16)
    behind_ref[...] = sums[2 * size :].astype(BF16)


def products(coefs, weights):
    return sum(
        lax.dot_general(
            coef_ref[...], weight_ref[...], CONTRACT_MIDDLE, preferred_element_type=F32
        )
        for coef_ref, weight_ref in zip(coefs, weights)
    )


def rest_kernel(
    own_rest_ref, sib_rest_ref, own_ref, sib_ref, own_power_ref, own_hot_ref, far_power_ref, far_hot_ref
):
    size = own_power_ref.shape[0]
    sums = products((own_rest_ref, sib_rest_ref), (own_ref, sib_ref))
    own_power_ref[...] = sums[:size]
    own_hot_ref[...] = sums[size : 2 * size].astype(BF16)
    far_power_ref[...] = sums[2 * size : 3 * size].astype(BF16)
    far_hot_ref[...] = sums[3 * size :].astype(BF16)


def merged(got_ref):
    senders = got_ref.shape[0]
    top = got_ref[0, 0:1, :]
    for k in range(1, senders):
        top = jnp.maximum(top, got_ref[k, 0:1, :])
    total, picked, weighted = [jnp.zeros_like(top)] * 3
    for k in range(senders):
        scale = jnp.exp(got_ref[k, 0:1, :] - top)
        total += got_ref[k, 1:2, :] * scale
        weighted += got_ref[k, 6:7, :] * scale
        picked += got_ref[k, 2:3, :]
    return top, total, picked, weighted


def merge_kernel(got_ref, own_ref, out_ref):
    top, total, picked, weighted = merged(got_ref)
    row = lax.broadcasted_iota(jnp.int32, own_ref.shape, 0)
    stats = own_ref[...]
    for i, value in ((0, top), (1, total), (2, picked), (6, weighted)):
        stats = jnp.where(row == i, value, stats)
    for k in range(out_ref.shape[0]):
        out_ref[k] = stats


def totals_kernel(got_ref, part_ref, dots_ref):
    rows, lanes = part_ref.shape
    top, total, picked, weighted = merged(got_ref)
    entries = got_ref[0]
    for k in range(1, got_ref.shape[0]):
        entries += got_ref[k]
    log_total = top + jnp.log(total)
    ratio = (picked - log_total - entries[3:4, :]) * entries[4:5, :]
    part_ref[...] = jnp.broadcast_to(jnp.sum(ratio, axis=1, keepdims=True), part_ref.shape)
    dots = jnp.broadcast_to(picked - weighted / total, (STAT_ROWS, lanes))
    dots_ref[...] = columns_of(by_distance(dots, rows)[0:1, :], rows)


def outer_kernel(
    got_ref, own_power_ref, own_hot_ref, ahead_ref, far_power_ref, far_hot_ref, behind_ref,
    out_ref, scale_ref, total_ref,
):
    size = own_power_ref.shape[0]
    rows = size // SIDE
    parts = out_ref.shape[0] // SIDE
    width = out_ref.shape[2]
    outer, inner = own_place()
    core = own_group()
    top, total, picked, _ = merged(got_ref)
    log_total = top + jnp.log(total)
    shape = got_ref.shape[1:]
    hot_factor = by_distance(jnp.broadcast_to(1.0 - jnp.exp(picked - log_total), shape), rows)
    scale_ref[SIDE] = columns_of(hot_factor[0:1, :], size)
    for k in range(SIDE):
        x, y = place_on(inner, (outer + SIDE - k) % SIDE, core)
        scale = jnp.exp(got_ref[y * SIDE + x] - log_total)
        scale_ref[k] = columns_of(by_distance(scale, rows)[5:6, :], size)
    for z in range(parts):
        for j in range(width // LANES):
            columns = slice(z * width + j * LANES, z * width + (j + 1) * LANES)
            power = scale_ref[0] * own_power_ref[:, columns]
            hot = own_hot_ref[:, columns].astype(F32)
            for k, block_ref in ((1, ahead_ref), (3, behind_ref)):
                power += scale_ref[k] * block_ref[:size, columns].astype(F32)
                hot += block_ref[size:, columns].astype(F32)
            power += scale_ref[2] * far_power_ref[:, columns].astype(F32)
            hot += far_hot_ref[:, columns].astype(F32)
            total_ref[:, j * LANES : (j + 1) * LANES] = scale_ref[SIDE] * hot - power
        for m in range(SIDE):
            term = total_ref[m * rows : (m + 1) * rows, :]
            out_ref[(inner + m) % SIDE * parts + z] = term.astype(out_ref.dtype)


def final_kernel(
    full_width, last_ref, hidden_ref, gain_ref, inv_ref, live_ref, dots_ref, own_part_ref,
    sib_part_ref, loss_ref, out_ref,
):
    rows, width = out_ref.shape
    term = last_ref[0].astype(F32)
    for k in range(1, last_ref.shape[0]):
        term += last_ref[k].astype(F32)
    own = pl.ds(pl.multiple_of(lax.axis_index("z") * width, width), width)
    value = -DPO_BETA * (own_part_ref[...] + sib_part_ref[...])
    loss = jnp.maximum(value, 0.0) + jnp.log1p(jnp.exp(-jnp.abs(value)))
    loss_ref[...] = loss[:1, :1]
    slope = -DPO_BETA / (1.0 + jnp.exp(-value))
    row_grad = (slope * live_ref[...])[:, :1]
    inv_rms = inv_ref[:, :1]
    row_dot = row_grad * (dots_ref[:, :1] / inv_rms) / full_width
    input_grad = inv_rms * (row_grad * (term * gain_ref[:, own])) - hidden_ref[...] * (
        inv_rms * inv_rms * inv_rms * row_dot
    )
    out_ref[...] = (LOSS_SCALE * input_grad).astype(out_ref.dtype)


def along_plane(value):
    groups = [
        [device(y, x, group) for y in range(SIDE) for x in range(SIDE)] for group in range(2)
    ]
    return lax.all_to_all(value, CTX, 0, 0, axis_index_groups=groups, tiled=True)


def along_inner_and_z(value, n_z):
    groups = [
        [
            device(*((inner, outer) if core == 0 else (outer, inner)), core) * n_z + z
            for inner in range(SIDE)
            for z in range(n_z)
        ]
        for core in range(2)
        for outer in range(SIDE)
    ]
    return lax.all_to_all(
        value, CTX + ("z",), 0, 0, axis_index_groups=groups, tiled=True
    )


def on_device(hidden, norm_gain, head_weight, targets, ref_logprobs, block_order, lengths):
    tok_dev, part_width = hidden.shape
    voc_dev, full_width = head_weight.shape
    n_plane = lax.axis_size(PLANE)
    n_z = lax.axis_size("z")
    half = tok_dev * n_plane
    block = half // SIDE
    rows_in_all = targets.shape[0]
    flops = 4 * half * voc_dev * full_width
    moved = 4 * (voc_dev + half) * full_width

    sib_weight = other_core(head_weight)
    sent, hidden_f32, gain, targets, live_rows, extra = run(
        prepare_kernel,
        [
            ((n_z * tok_dev, part_width), BF16),
            ((tok_dev, part_width), F32),
            ((1, full_width), F32),
            ((1, half), jnp.int32),
            ((tok_dev, LANES), F32),
            ((STAT_ROWS, half), F32),
        ],
        [
            pltpu.VMEM((tok_dev, part_width), BF16),
            pltpu.VMEM((1, rows_in_all), jnp.int32),
            pltpu.SMEM((tok_dev,), F32),
            pltpu.SMEM((2,), jnp.int32),
            pltpu.SMEM((2,), jnp.int32),
            pltpu.SemaphoreType.DMA((6,)),
        ],
        *[
            pltpu.with_memory_space_constraint(value, pltpu.HBM)
            for value in (
                hidden, norm_gain[None, :], targets[None, :], ref_logprobs, block_order, lengths
            )
        ],
        specs=[IN_HBM] * 6,
        moved=1 << 20,
    )
    sent = sent.reshape(n_z, tok_dev, part_width)

    features = exchange(sent, "z").astype(F32)
    normed, inv_rms = run(
        normed_kernel,
        [((tok_dev, full_width), BF16), ((tok_dev, LANES), F32)],
        [],
        features,
        gain,
        moved=2 * half * full_width,
    )
    normed, sib_weight = lax.optimization_barrier((normed, sib_weight))
    sib_weight = pltpu.with_memory_space_constraint(sib_weight, pltpu.VMEM)
    nearby = gather_from(normed, False)
    ahead = from_ahead(nearby, 1, True)
    ahead, own_weight = lax.optimization_barrier((ahead, head_weight))
    (own_weight,) = run(
        load_kernel,
        [((voc_dev, full_width), BF16)],
        [pltpu.SemaphoreType.DMA((full_width // CHUNK,))],
        pltpu.with_memory_space_constraint(own_weight, pltpu.HBM),
        specs=[IN_HBM],
        moved=4 * voc_dev * full_width,
    )
    rows = jnp.concatenate(
        [
            nearby,
            ahead,
            from_ahead(nearby[: block // 2], 2, True),
            from_ahead(nearby[block // 2 :], 2, True),
            from_ahead(nearby, 3, True),
        ],
        axis=0,
    )
    own_logits, sib_logits, stats, tops, own_stats = run(
        functools.partial(logits_kernel, n_z),
        [
            ((voc_dev, half), F32),
            ((voc_dev, half), F32),
            ((n_z, STAT_ROWS, half), F32),
            ((STAT_ROWS, half), F32),
            ((STAT_ROWS, half), F32),
        ],
        [],
        rows,
        own_weight,
        sib_weight,
        targets,
        extra,
        flops=flops,
        moved=moved,
    )
    ahead, behind, own_rest, sib_rest = run(
        functools.partial(sums_kernel, n_z),
        [((2 * block, full_width), BF16)] * 2 + [((half, voc_dev), BF16)] * 2,
        [pltpu.VMEM((half, voc_dev), BF16)] * 2,
        own_logits,
        sib_logits,
        tops,
        targets,
        own_weight,
        sib_weight,
        flops=flops,
        moved=moved,
    )
    ahead, behind = from_ahead(ahead, 3, True), from_ahead(behind, 1, True)
    own_power, own_hot, far_power, far_hot = run(
        rest_kernel,
        [((block, full_width), F32)] + [((block, full_width), BF16)] * 3,
        [],
        own_rest,
        sib_rest,
        own_weight,
        sib_weight,
        flops=flops,
        moved=moved,
    )
    stats, far_power, far_hot = lax.optimization_barrier((stats, far_power, far_hot))
    far_power, far_hot = [from_ahead(far, 2, True) for far in (far_power, far_hot)]
    (stats,) = run(
        merge_kernel,
        [((n_plane, STAT_ROWS, half), F32)],
        [],
        exchange(stats, "z"),
        own_stats,
        moved=1 << 17,
    )
    got = along_plane(stats)
    own_part, dots = run(
        totals_kernel, [((tok_dev, LANES), F32)] * 2, [], got, moved=1 << 17
    )
    sib_part = other_core(own_part)
    (last,) = run(
        outer_kernel,
        [((SIDE * n_z, tok_dev, part_width), BF16)],
        [pltpu.VMEM((SIDE + 1, block, half), F32), pltpu.VMEM((block, part_width), F32)],
        got,
        own_power,
        own_hot,
        ahead,
        far_power,
        far_hot,
        behind,
        moved=8 * half * full_width,
    )
    last, sib_part = lax.optimization_barrier((last, sib_part))
    last = along_inner_and_z(last, n_z)
    loss, hidden_grad = pl.pallas_call(
        functools.partial(final_kernel, full_width),
        in_specs=[IN_VMEM] * 8,
        out_specs=[IN_VMEM] * 2,
        out_shape=[
            jax.ShapeDtypeStruct((1, 1), F32),
            jax.ShapeDtypeStruct((tok_dev, part_width), BF16),
        ],
        compiler_params=pltpu.CompilerParams(vmem_limit_bytes=VMEM_LIMIT),
    )(last, hidden_f32, gain, inv_rms, live_rows, dots, own_part, sib_part)
    return (loss[0, 0], hidden_grad)


def solution(mesh):
    fine = Mesh(mesh.devices.reshape(SIDE, SIDE, 2, 8), ("y", "x", "c", "z"))
    placed = (P(CTX, "z"), P(), P(CTX + ("z",), None), P(), P(CTX), P(CTX), P())
    return jax.shard_map(
        on_device, mesh=fine, in_specs=placed, out_specs=(P(), P(CTX, "z")), check_vma=False
    )
```
